128 devices in a mesh: gx: 8 (over y, x_hi), gy: 8 (over z, core), gz: 2 (over x_lo).
Axes of the slice: x: 4 (x_hi: 2, x_lo: 2; x = x_hi * 2 + x_lo), y: 4, z: 4, core: 2. Of those that a mesh axis runs over, the one named last changes fastest.
Arguments:
- strength: bfloat16 [3, 1048576], P(None, ('gx', 'gy', 'gz')), may hold values from -6 to 6
- fraction: float32 [3, 1048576], P(None, ('gx', 'gy', 'gz')), may hold values from 0 to 1
- stream_cell: int32 [1048576], P(('gx', 'gy', 'gz')), may hold values from -2 to 64
- span_cell: int32 [1048576], P(('gx', 'gy', 'gz')), may hold values from -2 to 32
- height_cell: int32 [1048576], P(('gx', 'gy', 'gz')), may hold values from -2 to 128
- velocity: float32 [3, 512, 256, 256], P(None, 'gx', 'gy', 'gz'), may hold values from -6 to 6
Outputs:
- vorticity: float32 [3, 512, 256, 256], P(None, 'gx', 'gy', 'gz')
The draws below stay inside these ranges and needn't reach their ends.
All inputs are finite; a program needn't handle non-finite values.
Results may differ from the reference program's by a relative error of at most 0.0036.
Values sent between devices are 32-bit elements; how exact they have to be, the bound alone decides.
No kernel may reach another device: no remote copies, remote signals or barrier semaphores. Data moves between devices by JAX's collectives and lax.ppermute only.
A program may use at most 192 MiB of HBM per device.

```python
import jax
import jax.numpy as jnp
from jax import lax

CX = 64
CY = 32
CZ = 128
PART_DEV = 8192
NX = 512
NY = 256
NZ = 256
PARTICLES = 1048576
N_GY = 8
N_GZ = 2


def place_ends(values, key, smallest, largest):
    longest = values.shape.index(max(values.shape))
    spots = []
    for shift in (0, 1):
        where = [jax.random.randint(jax.random.fold_in(key, axis), (), 0, length) for axis, length in enumerate(values.shape)]
        where[longest] = (where[longest] + shift) % values.shape[longest]
        spots.append(tuple(where))
    return values.at[spots[0]].set(smallest).at[spots[1]].set(largest)


def block_scale(rng, extent, cuts, low, high):
    def one(position, parts):
        draws = jax.random.uniform(jax.random.fold_in(jax.random.fold_in(rng, 6), position), (parts,), jnp.float32, low / len(cuts), high / len(cuts))
        return jnp.repeat(jnp.exp(draws), extent[position] // parts).reshape((-1,) + (1,) * (len(extent) - position - 1))

    loudness = one(*cuts[0])
    for cut in cuts[1:]:
        loudness = loudness * one(*cut)
    return loudness


def scatter_about(key, extent, spread, most, cuts=(), held_as=jnp.bfloat16):
    entries = spread * jax.random.normal(key, extent, jnp.float32)
    if cuts:
        entries = entries * block_scale(key, extent, cuts, -0.22, 0.18)
    return jnp.clip(entries, -most, most).astype(held_as)


def setup_inputs(seed: int = 0) -> dict:
    keys = jax.random.split(jax.random.key(seed), 7)
    return {
        "strength": scatter_about(keys[0], (3, PARTICLES), 1.0, 6.0, ((1, 128),)),
        "fraction": jnp.clip(1.0 * jax.random.uniform(keys[1], (3, PARTICLES), jnp.float32) ** block_scale(keys[1], (3, PARTICLES), ((1, 128),), -0.2, 0.2), 0.0, 1.0),
        "stream_cell": place_ends(jax.random.randint(keys[2], (PARTICLES,), -2, CX + 1), jax.random.fold_in(keys[2], 1), -2, CX).astype(jnp.int32),
        "span_cell": place_ends(jax.random.randint(keys[3], (PARTICLES,), -2, CY + 1), jax.random.fold_in(keys[3], 1), -2, CY).astype(jnp.int32),
        "height_cell": place_ends(jax.random.randint(keys[4], (PARTICLES,), -2, CZ + 1), jax.random.fold_in(keys[4], 1), -2, CZ).astype(jnp.int32),
        "velocity": scatter_about(keys[5], (3, NX, NY, NZ), 1.0, 6.0, ((1, 8), (2, 8), (3, 2)), jnp.float32),
    }


time_step = 0.1
viscosity = 0.5


def kernel_weights(fraction):
    remainder = 1.0 - fraction
    return jnp.stack([
        -0.5 * fraction * remainder * remainder,
        1.0 - 2.5 * fraction * fraction + 1.5 * fraction * fraction * fraction,
        1.0 - 2.5 * remainder * remainder + 1.5 * remainder * remainder * remainder,
        -0.5 * fraction * fraction * remainder,
    ])


def shifted(source, dimension, offset):
    window = [slice(None)] + [slice(2, source.shape[spatial] - 2) for spatial in (1, 2, 3)]
    window[dimension] = slice(2 + offset, source.shape[dimension] - 2 + offset)
    return source[tuple(window)]


def advance(swirl, moving):
    centre = shifted(swirl, 1, 0)
    laplace = jnp.zeros_like(centre)
    stretch = jnp.zeros_like(centre)
    for dimension in (1, 2, 3):
        laplace = laplace + (16.0 * (shifted(swirl, dimension, 1) + shifted(swirl, dimension, -1))
                             - (shifted(swirl, dimension, 2) + shifted(swirl, dimension, -2)) - 30.0 * centre) / 12.0
        slope = (8.0 * (shifted(moving, dimension, 1) - shifted(moving, dimension, -1))
                 - (shifted(moving, dimension, 2) - shifted(moving, dimension, -2))) / 12.0
        stretch = stretch + centre[dimension - 1][None] * slope
    return centre + time_step * (stretch + viscosity * laplace)


def pad_mesh(source):
    return jnp.pad(source, ((0, 0), (2, 2), (2, 2), (2, 2)))


def reference(strength, fraction, stream_cell, span_cell, height_cell, velocity):
    owners = jnp.arange(PARTICLES, dtype=jnp.int32) // PART_DEV
    brick_x = owners // (N_GY * N_GZ)
    brick_y = (owners // N_GZ) % N_GY
    brick_z = owners % N_GZ
    place_x = brick_x * CX + stream_cell + 2
    place_y = brick_y * CY + span_cell + 2
    place_z = brick_z * CZ + height_cell + 2
    weights_x = kernel_weights(fraction[0])
    weights_y = kernel_weights(fraction[1])
    weights_z = kernel_weights(fraction[2])
    source = strength.astype(jnp.float32)

    def deposit(shift_code, grid):
        step_x = shift_code // 16
        step_y = (shift_code // 4) % 4
        step_z = shift_code % 4
        lead = (source * weights_x[step_x][None]).astype(jnp.bfloat16)
        cross = (weights_y[step_y] * weights_z[step_z]).astype(jnp.bfloat16)
        lead, cross = lax.optimization_barrier((lead, cross))
        term = lead.astype(jnp.float32) * cross.astype(jnp.float32)[None]
        return grid.at[:, place_x + step_x, place_y + step_y, place_z + step_z].add(term)

    grid = jnp.zeros((3, NX + 6, NY + 6, NZ + 6), jnp.float32)
    grid = lax.fori_loop(0, 64, deposit, grid)
    remeshed = grid[:, 3:NX + 3, 3:NY + 3, 3:NZ + 3]
    moving = pad_mesh(velocity)
    first = advance(pad_mesh(remeshed), moving)
    return advance(pad_mesh(first), moving)
```

```python
import functools

import jax
import jax.numpy as jnp
from jax import lax
from jax.experimental import pallas as pl
from jax.experimental.pallas import tpu as pltpu
from jax.sharding import PartitionSpec as P

GROUP = 80
ROWS = 240
PLANES = 40
DEPTH = 144
WINDOW = 6


def kernel_weights(fraction):
    remainder = 1.0 - fraction
    return (
        -0.5 * fraction * remainder * remainder,
        1.0 - 2.5 * fraction * fraction + 1.5 * fraction * fraction * fraction,
        1.0 - 2.5 * remainder * remainder + 1.5 * remainder * remainder * remainder,
        -0.5 * fraction * fraction * remainder,
    )


def choose(distance, weights):
    total = jnp.where(distance == 3, weights[3], 0.0)
    for offset in (2, 1, 0):
        total = jnp.where(distance == offset, weights[offset], total)
    return total


def add_source(bounds_ref, number, ref, shift, grid_ref):
    rows_x = lax.broadcasted_iota(jnp.int32, (GROUP, 128), 0)
    rows_z = lax.broadcasted_iota(jnp.int32, (DEPTH, 128), 0)

    def group(turn, carry):
        field = [ref[pl.ds(64 * f + 8 * turn, 8), :] for f in range(9)]
        weight_x = kernel_weights(field[3])
        weight_y = kernel_weights(field[4])
        weight_z = kernel_weights(field[5])
        cell_x = field[6].astype(jnp.int32) + (7 + shift)
        cell_y = field[7].astype(jnp.int32) + 3
        cell_z = field[8].astype(jnp.int32) + 7
        low = [bounds_ref[number, 0, 4 * turn + k] + 3 for k in range(4)]
        high = [bounds_ref[number, 1, 4 * turn + k] + 6 for k in range(4)]
        turns = functools.reduce(
            jnp.maximum, [(high[k] - low[k] + WINDOW) // WINDOW for k in range(4)]
        )

        def window(step, inner):
            for k in range(4):
                base = jnp.minimum(low[k] + step * WINDOW, 39)
                leads, ups, rows = [], [], []
                for half in (2 * k, 2 * k + 1):
                    row = slice(half, half + 1)
                    spread_x = choose(rows_x - cell_x[row], [w[row] for w in weight_x])
                    spread_z = choose(rows_z - cell_z[row], [w[row] for w in weight_z])
                    leads.append(
                        jnp.concatenate(
                            [(field[c][row] * spread_x).astype(jnp.bfloat16) for c in range(3)]
                            + [jnp.zeros((16, 128), jnp.bfloat16)],
                            0,
                        )
                    )
                    ups.append(spread_z)
                    rows.append(
                        [
                            choose(base + j - cell_y[row], [w[row] for w in weight_y])
                            for j in range(WINDOW)
                        ]
                    )
                lead = jnp.concatenate(leads, 1)
                for j in range(WINDOW):
                    cross = jnp.concatenate(
                        [(rows[h][j] * ups[h]).astype(jnp.bfloat16) for h in range(2)], 1
                    )
                    product = lax.dot_general(
                        cross, lead, (((1,), (1,)), ((), ())),
                        preferred_element_type=jnp.float32,
                    )
                    for half in range(2):
                        grid_ref[base + j, half] += product[:, 128 * half : 128 * half + 128]
            return inner

        lax.fori_loop(0, turns, window, 0)
        return carry

    lax.fori_loop(0, 8, group, 0)


def own_kernel(bounds_ref, own_ref, grid_ref):
    grid_ref[...] = jnp.zeros_like(grid_ref)
    add_source(bounds_ref, 0, own_ref, 0, grid_ref)


def neighbour_kernel(bounds_ref, low_ref, high_ref, start_ref, grid_ref):
    grid_ref[...] = start_ref[...]
    add_source(bounds_ref, 0, low_ref, -64, grid_ref)
    add_source(bounds_ref, 1, high_ref, 64, grid_ref)


GRID = jax.ShapeDtypeStruct((PLANES + 5, 2, DEPTH, 128), jnp.float32)


def deposit_own(bounds, own):
    vmem = pl.BlockSpec(memory_space=pltpu.VMEM)
    smem = pl.BlockSpec(memory_space=pltpu.SMEM)
    return pl.pallas_call(
        own_kernel,
        out_shape=GRID,
        in_specs=[smem, vmem],
        out_specs=vmem,
        compiler_params=pltpu.CompilerParams(vmem_limit_bytes=32 * 1024 * 1024),
        cost_estimate=pl.CostEstimate(
            flops=8_000_000_000, bytes_accessed=40_000_000, transcendentals=0
        ),
        name="deposit_own",
    )(bounds, own)


def deposit_neighbours(bounds, low, high, grid):
    vmem = pl.BlockSpec(memory_space=pltpu.VMEM)
    smem = pl.BlockSpec(memory_space=pltpu.SMEM)
    return pl.pallas_call(
        neighbour_kernel,
        out_shape=GRID,
        in_specs=[smem, vmem, vmem, vmem],
        out_specs=vmem,
        compiler_params=pltpu.CompilerParams(vmem_limit_bytes=40 * 1024 * 1024),
        name="deposit_neighbours",
    )(bounds, low, high, grid)


def velocity_kernel(side_ref, main_ref, low_ref, high_ref, out_ref, slab_ref):
    upper = side_ref[0] == 0
    lane = lax.broadcasted_iota(jnp.int32, (ROWS, 128), 1)
    first = jnp.where(upper, 124, 0)
    target = jnp.where(upper, 0, 4)
    zeros = jnp.zeros((8, 128), jnp.float32)
    for turn in range(2):

        def plane(k, gathered):
            y = 16 * turn + k
            pieces = []
            for c in range(3):
                start = GROUP * c
                out_ref[y, start : start + 8] = zeros
                out_ref[y, start + 72 : start + 80] = zeros
                out_ref[y, start + 8 : start + 72] = main_ref[pl.ds(2048 * c + y, 64, stride=32), :]
                out_ref[y, start + 4 : start + 8] = low_ref[pl.ds(576 + 128 * c + y, 4, stride=32), :]
                out_ref[y, start + 72 : start + 76] = high_ref[pl.ds(576 + 128 * c + y, 4, stride=32), :]
            goal = 8 * k + target
            moved = pltpu.roll(out_ref[y], (goal - first + 128) % 128, 1)
            return jnp.where((lane >= goal) & (lane < goal + 4), moved, gathered)

        gathered = lax.fori_loop(0, 16, plane, jnp.zeros((ROWS, 128), jnp.float32))
        padded = jnp.concatenate([gathered, jnp.zeros((256 - ROWS, 128), jnp.float32)], 0)
        slabs = jnp.transpose(padded)
        for half in range(2):
            slab_ref[16 * turn : 16 * turn + 16, half] = slabs[
                :, 128 * half : 128 * half + 128
            ].reshape(16, 8, 128)


def arrange_velocity(side, main, low, high):
    vmem = pl.BlockSpec(memory_space=pltpu.VMEM)
    smem = pl.BlockSpec(memory_space=pltpu.SMEM)
    return pl.pallas_call(
        velocity_kernel,
        out_shape=(
            jax.ShapeDtypeStruct((32, ROWS, 128), jnp.float32),
            jax.ShapeDtypeStruct((32, 2, 8, 128), jnp.float32),
        ),
        in_specs=[smem, vmem, vmem, vmem],
        out_specs=(vmem, vmem),
        compiler_params=pltpu.CompilerParams(vmem_limit_bytes=32 * 1024 * 1024),
        name="arrange_velocity",
    )(side, main, low, high)


def bands(upper, odd):
    source = lax.broadcasted_iota(jnp.int32, (128, 128), 0)
    target = lax.broadcasted_iota(jnp.int32, (128, 128), 1)

    def entries(distance):
        near = jnp.where(distance == 1, 8.0 if odd else 16.0, 0.0)
        near = jnp.where(distance == -1, -8.0 if odd else 16.0, near)
        near = jnp.where(distance == 2, -1.0, near)
        return jnp.where(distance == -2, 1.0 if odd else -1.0, near)

    main = entries(source - target).astype(jnp.bfloat16)
    layer = source % 8
    begin = jnp.where(upper, 4, 0)
    outer = (layer >= begin) & (layer < begin + 4)
    halo = jnp.where(outer, entries(layer + jnp.where(upper, 124, -4) - target), 0.0)
    return main, halo, source // 8


def stencil_kernel(
    place_ref, grid_ref, slab_ref, speed_ref, speed_slab_ref, low_ref, high_ref,
    out_ref, w_ref, wt_ref, a_ref, v_ref, vt_ref, b_ref, f_ref, e_ref, even_ref, odd_ref, d_ref,
):
    first_x, last_x = place_ref[0] == 0, place_ref[0] == place_ref[1] - 1
    first_y, last_y = place_ref[2] == 0, place_ref[2] == place_ref[3] - 1
    upper = place_ref[4] == 0
    start_x, stop_x = jnp.where(first_x, 8, 0), jnp.where(last_x, 72, GROUP)
    row = lax.broadcasted_iota(jnp.int32, (GROUP, 128), 0)
    inside = jnp.where((row >= start_x) & (row < stop_x), 1.0, 0.0)
    lane = lax.broadcasted_iota(jnp.int32, (8, 256), 1)
    column = lane % GROUP
    inside_slab = jnp.where((column >= start_x) & (column < stop_x), 1.0, 0.0)
    inside_slab = jnp.where(lane < ROWS, inside_slab, 0.0)
    layer = lax.broadcasted_iota(jnp.int32, (8, 256), 0)
    keep_low = jnp.where(first_y, 0.0, 1.0)
    keep_high = jnp.where(last_y, 0.0, 1.0)
    zeros = jnp.zeros((8, 128), jnp.float32)

    for odd, ref in ((False, even_ref), (True, odd_ref)):
        main, halo, owner = bands(upper, odd)
        for k in range(16):
            ref[k, 0:128] = main
            ref[k, 128:256] = jnp.where(owner == k, halo, 0.0).astype(jnp.bfloat16)

    def place(plane, main, slab):
        slab = slab * inside_slab
        a_ref[plane] = slab
        inner = pltpu.roll(slab, 4, 0)
        bottom = jnp.where((layer < 4) & (layer < jnp.where(upper, 0, 8)), inner, main[0:8] * inside_slab)
        top = jnp.where((layer >= 4) & (layer < jnp.where(upper, 8, 0)), inner, main[120:128] * inside_slab)
        block = jnp.concatenate([bottom, main[8:120], top], 0)
        turned = jnp.transpose(block)
        w_ref[plane, 0:8] = zeros
        w_ref[plane, 248:256] = zeros
        for c in range(3):
            w_ref[plane, 8 + GROUP * c : 88 + GROUP * c] = turned[GROUP * c : GROUP * c + GROUP] * inside

    def joined(ref, plane, start, stop):
        return jnp.concatenate([ref[plane, 0, start:stop], ref[plane, 1, start:stop]], 1)

    def received(ref, k, start, stop):
        base = 272 * k
        return jnp.concatenate(
            [ref[base + start : base + stop], ref[base + 136 + start : base + 136 + stop]], 1
        )

    for ref, begin, outside, keep in ((low_ref, 0, 4, keep_low), (high_ref, 33, 4, keep_high)):
        for k in range(7):
            plane = begin + k
            beyond = k < 4 if begin == 0 else k >= 3
            scale = keep if beyond else 1.0
            place(
                plane,
                (joined(grid_ref, plane, 8, 136) + received(ref, k, 0, 128)) * scale,
                (joined(slab_ref, plane, 0, 8) + received(ref, k, 128, 136)) * scale,
            )

    def middle(plane, carry):
        place(plane, joined(grid_ref, plane, 8, 136), joined(slab_ref, plane, 0, 8))
        return carry

    lax.fori_loop(7, 33, middle, 0, unroll=2)

    def place_speed(plane, main, slab):
        v_ref[plane, 0:8] = zeros
        v_ref[plane, 248:256] = zeros
        v_ref[plane, 8:248] = main
        b_ref[plane] = slab

    for ref, begin in ((low_ref, 0), (high_ref, 36)):
        for k in range(4):
            start = 1904 + 240 * k
            end = 2864 + 16 * k
            place_speed(
                begin + k,
                ref[start : start + 240],
                jnp.concatenate([ref[end : end + 8], ref[end + 8 : end + 16]], 1),
            )

    def middle_speed(plane, carry):
        place_speed(plane + 4, speed_ref[plane], joined(speed_slab_ref, plane, 0, 8))
        return carry

    lax.fori_loop(0, 32, middle_speed, 0)

    def turn_slabs(source_ref, target_ref, groups):
        for g in range(groups):
            planes = [source_ref[16 * g + k] for k in range(16)]
            stacked = jnp.concatenate(planes, 0)
            target_ref[g] = jnp.transpose(stacked)[:ROWS].astype(jnp.bfloat16)

    blank = jnp.zeros((8, 256), jnp.float32)
    for k in range(40, 48):
        a_ref[k] = blank
        b_ref[k] = blank
    turn_slabs(a_ref, wt_ref, 3)
    turn_slabs(b_ref, vt_ref, 3)

    scale_l = 0.1 * 0.5 / 12.0
    scale_d = 0.1 / 12.0

    def along_z(main, halo, matrix):
        return jnp.dot(
            jnp.concatenate([main.astype(jnp.bfloat16), halo], 1), matrix,
            preferred_element_type=jnp.float32,
        )

    def part(array_ref, plane, c, dx):
        start = 8 + GROUP * c + dx
        return array_ref[plane, start : start + GROUP]

    def curvature(ref, y, c):
        near = (
            part(ref, y + 1, c, 0) + part(ref, y - 1, c, 0)
            + (part(ref, y, c, 1) + part(ref, y, c, -1))
        )
        far = (
            part(ref, y + 2, c, 0) + part(ref, y - 2, c, 0)
            + (part(ref, y, c, 2) + part(ref, y, c, -2))
        )
        return 16.0 * near - far

    def first_step(k, carry):
        y = k + 2
        scale = jnp.where(k < 2, keep_low, jnp.where(k >= 34, keep_high, 1.0))
        curve = along_z(w_ref[y, 8:248], wt_ref[y >> 4], even_ref[y & 15])
        climb = along_z(v_ref[y, 8:248], vt_ref[y >> 4], odd_ref[y & 15])
        f_ref[k, 0:8] = zeros
        f_ref[k, 248:256] = zeros
        centre = [part(w_ref, y, c, 0) for c in range(3)]
        for c in range(3):
            rows = slice(GROUP * c, GROUP * c + GROUP)
            slope_x = 8.0 * (part(v_ref, y, c, 1) - part(v_ref, y, c, -1)) - (
                part(v_ref, y, c, 2) - part(v_ref, y, c, -2)
            )
            slope_y = 8.0 * (part(v_ref, y + 1, c, 0) - part(v_ref, y - 1, c, 0)) - (
                part(v_ref, y + 2, c, 0) - part(v_ref, y - 2, c, 0)
            )
            d_ref[k, 0, rows] = slope_x
            d_ref[k, 1, rows] = slope_y
            d_ref[k, 2, rows] = climb[rows]
            stretch = centre[0] * slope_x + centre[1] * slope_y + centre[2] * climb[rows]
            result = (
                centre[c] * (1.0 - 90.0 * scale_l)
                + scale_l * (curvature(w_ref, y, c) + curve[rows])
                + scale_d * stretch
            )
            f_ref[k, 8 + GROUP * c : 88 + GROUP * c] = result * (inside * scale)
        return carry

    lax.fori_loop(0, 36, first_step, 0, unroll=2)

    group = lane // GROUP

    def slab_step(k, carry):
        y = k + 4
        here = a_ref[y]
        speed = b_ref[y]

        def both_ways(array, step, axis):
            size = array.shape[axis]
            return pltpu.roll(array, size - step, axis), pltpu.roll(array, step, axis)

        ax1, bx1 = both_ways(here, 1, 1)
        ax2, bx2 = both_ways(here, 2, 1)
        az1, bz1 = both_ways(here, 1, 0)
        az2, bz2 = both_ways(here, 2, 0)
        near = a_ref[y + 1] + a_ref[y - 1] + (ax1 + bx1) + (az1 + bz1)
        far = a_ref[y + 2] + a_ref[y - 2] + (ax2 + bx2) + (az2 + bz2)
        vx1, ux1 = both_ways(speed, 1, 1)
        vx2, ux2 = both_ways(speed, 2, 1)
        vz1, uz1 = both_ways(speed, 1, 0)
        vz2, uz2 = both_ways(speed, 2, 0)
        slope_x = 8.0 * (vx1 - ux1) - (vx2 - ux2)
        slope_y = 8.0 * (b_ref[y + 1] - b_ref[y - 1]) - (b_ref[y + 2] - b_ref[y - 2])
        slope_z = 8.0 * (vz1 - uz1) - (vz2 - uz2)
        right1 = pltpu.roll(here, GROUP, 1)
        right2 = pltpu.roll(here, 2 * GROUP, 1)
        left1 = pltpu.roll(here, 256 - GROUP, 1)
        left2 = pltpu.roll(here, 256 - 2 * GROUP, 1)
        swirl_x = jnp.where(group == 0, here, jnp.where(group == 1, right1, right2))
        swirl_y = jnp.where(group == 0, left1, jnp.where(group == 1, here, right1))
        swirl_z = jnp.where(group == 0, left2, jnp.where(group == 1, left1, here))
        e_ref[k] = (
            here * (1.0 - 90.0 * scale_l)
            + scale_l * (16.0 * near - far)
            + scale_d * (swirl_x * slope_x + swirl_y * slope_y + swirl_z * slope_z)
        )
        return carry

    lax.fori_loop(0, 32, slab_step, 0, unroll=2)
    turn_slabs(e_ref, vt_ref, 2)

    def second_step(k, carry):
        y = k + 2
        curve = along_z(f_ref[y, 8:248], vt_ref[k >> 4], even_ref[k & 15])
        centre = [part(f_ref, y, c, 0) for c in range(3)]
        for c in range(3):
            rows = slice(GROUP * c, GROUP * c + GROUP)
            stretch = (
                centre[0] * d_ref[y, 0, rows]
                + centre[1] * d_ref[y, 1, rows]
                + centre[2] * d_ref[y, 2, rows]
            )
            result = (
                centre[c] * (1.0 - 90.0 * scale_l)
                + scale_l * (curvature(f_ref, y, c) + curve[rows])
                + scale_d * stretch
            )
            out_ref[pl.ds(2048 * c + k, 64, stride=32), :] = result[8:72]
        return carry

    lax.fori_loop(0, 32, second_step, 0, unroll=2)


def stencils(place, grid, slab, speed, speed_slab, low, high):
    vmem = pl.BlockSpec(memory_space=pltpu.VMEM)
    smem = pl.BlockSpec(memory_space=pltpu.SMEM)
    scratch = [
        pltpu.VMEM((PLANES, 256, 128), jnp.float32),
        pltpu.VMEM((3, ROWS, 128), jnp.bfloat16),
        pltpu.VMEM((48, 8, 256), jnp.float32),
        pltpu.VMEM((PLANES, 256, 128), jnp.float32),
        pltpu.VMEM((3, ROWS, 128), jnp.bfloat16),
        pltpu.VMEM((48, 8, 256), jnp.float32),
        pltpu.VMEM((36, 256, 128), jnp.float32),
        pltpu.VMEM((32, 8, 256), jnp.float32),
        pltpu.VMEM((16, 256, 128), jnp.bfloat16),
        pltpu.VMEM((16, 256, 128), jnp.bfloat16),
        pltpu.VMEM((36, 3, ROWS, 128), jnp.float32),
    ]
    return pl.pallas_call(
        stencil_kernel,
        out_shape=jax.ShapeDtypeStruct((3 * 64 * 32, 128), jnp.float32),
        in_specs=[smem] + [vmem] * 6,
        out_specs=vmem,
        scratch_shapes=scratch,
        compiler_params=pltpu.CompilerParams(vmem_limit_bytes=58 * 1024 * 1024),
        name="stencils",
    )(place, grid, slab, speed, speed_slab, low, high)


def sort_inputs(strength, fraction, stream_cell, span_cell, height_cell):
    key = ((span_cell + 2) << 16) | ((stream_cell + 2) << 8) | (height_cell + 2)
    load = strength.astype(jnp.float32)
    return lax.sort(
        (key, load[0], load[1], load[2], fraction[0], fraction[1], fraction[2]),
        num_keys=1, is_stable=False,
    )


def pack_kernel(key_ref, *refs):
    fields, velocity_ref, up_ref, down_ref = refs[:6], refs[6], refs[7], refs[8]
    key = key_ref[...]
    cells = ((key >> 8) & 255, key >> 16, key & 255)
    for target in (up_ref, down_ref):
        for f in range(6):
            target[64 * f : 64 * f + 64] = fields[f][...]
        for f in range(3):
            target[384 + 64 * f : 448 + 64 * f] = (cells[f] - 2).astype(jnp.float32)
    for c in range(3):
        start = 576 + 128 * c
        up_ref[start : start + 128] = velocity_ref[2048 * c + 1920 : 2048 * c + 2048]
        down_ref[start : start + 128] = velocity_ref[2048 * c : 2048 * c + 128]


def pack(parts, velocity):
    vmem = pl.BlockSpec(memory_space=pltpu.VMEM)
    return pl.pallas_call(
        pack_kernel,
        out_shape=(jax.ShapeDtypeStruct((960, 128), jnp.float32),) * 2,
        in_specs=[vmem] * 8,
        out_specs=(vmem, vmem),
        compiler_params=pltpu.CompilerParams(vmem_limit_bytes=16 * 1024 * 1024),
        name="pack",
    )(*[p.reshape(64, 128) for p in parts], velocity)


def shards(strength, fraction, stream_cell, span_cell, height_cell, velocity):
    count_x, count_y = lax.axis_size("gx"), lax.axis_size("gy")
    index_x, index_y, index_z = (lax.axis_index(a) for a in ("gx", "gy", "gz"))
    side = index_z.astype(jnp.int32).reshape(1)
    place = jnp.stack(
        [index_x, jnp.int32(count_x), index_y, jnp.int32(count_y), index_z]
    ).astype(jnp.int32)
    velocity = velocity.reshape(6144, 128)
    parts = sort_inputs(strength, fraction, stream_cell, span_cell, height_cell)
    upward, downward = pack(parts, velocity)

    up_x = [(i, i + 1) for i in range(count_x - 1)]
    up_y = [(i, i + 1) for i in range(count_y - 1)]
    low = lax.ppermute(upward, "gx", up_x)
    high = lax.ppermute(downward, "gx", [(j, i) for i, j in up_x])

    def limits(block):
        span = block[448:512].reshape(32, 256)
        return jnp.stack([span[:, 0], span[:, 255]]).astype(jnp.int32)

    grid = deposit_own(limits(upward)[None], upward)
    grid = deposit_neighbours(jnp.stack([limits(low), limits(high)]), low, high, grid)
    speed, speed_slab = arrange_velocity(side, velocity, low, high)
    upper = index_z == 0
    slab = jnp.where(upper, grid[:PLANES, :, 132:140], grid[:PLANES, :, 4:12])
    swapped = lax.ppermute(
        jnp.concatenate([slab, speed_slab], 0), "gz", [(0, 1), (1, 0)]
    )
    slab = slab + swapped[:PLANES]
    speed_slab = speed_slab + swapped[PLANES:]

    def face(start, start_speed):
        swirl = jnp.concatenate(
            [grid[start : start + 7, :, 8:136], slab[start : start + 7]], 2
        )
        return jnp.concatenate(
            [
                swirl.reshape(1904, 128),
                speed[start_speed : start_speed + 4].reshape(960, 128),
                speed_slab[start_speed : start_speed + 4].reshape(64, 128),
            ],
            0,
        )

    from_low = lax.ppermute(face(32, 28), "gy", up_y)
    from_high = lax.ppermute(face(1, 0), "gy", [(j, i) for i, j in up_y])
    out = stencils(place, grid, slab, speed, speed_slab, from_low, from_high)
    return out.reshape(3, 64, 32, 128)


def solution(mesh):
    return jax.shard_map(
        shards,
        mesh=mesh,
        in_specs=(
            P(None, ("gx", "gy", "gz")),
            P(None, ("gx", "gy", "gz")),
            P(("gx", "gy", "gz")),
            P(("gx", "gy", "gz")),
            P(("gx", "gy", "gz")),
            P(None, "gx", "gy", "gz"),
        ),
        out_specs=P(None, "gx", "gy", "gz"),
        check_vma=False,
    )
```

```python
import functools

import jax
import jax.numpy as jnp
from jax import lax
from jax.experimental import pallas as pl
from jax.experimental.pallas import tpu as pltpu
from jax.sharding import PartitionSpec as P

GROUP = 80
ROWS = 240
PLANES = 40
DEPTH = 144
WINDOW = 10
LAYERS = DEPTH + 5


def kernel_weights(fraction):
    remainder = 1.0 - fraction
    return (
        -0.5 * fraction * remainder * remainder,
        1.0 - 2.5 * fraction * fraction + 1.5 * fraction * fraction * fraction,
        1.0 - 2.5 * remainder * remainder + 1.5 * remainder * remainder * remainder,
        -0.5 * fraction * fraction * remainder,
    )


def choose(distance, weights):
    total = jnp.where(distance == 3, weights[3], 0.0)
    for offset in (2, 1, 0):
        total = jnp.where(distance == offset, weights[offset], total)
    return total


def add_source(bounds_ref, number, ref, shift, grid_ref):
    start_x, count_x = {0: (0, GROUP), -64: (0, 16), 64: (64, 16)}[shift]
    rows_x = lax.broadcasted_iota(jnp.int32, (count_x, 128), 0) + start_x
    below = jnp.zeros((start_x, 128), jnp.bfloat16)
    above = jnp.zeros((GROUP - start_x - count_x, 128), jnp.bfloat16)
    rows_y = lax.broadcasted_iota(jnp.int32, (PLANES, 128), 0)
    owner = lax.broadcasted_iota(jnp.int32, (8, 128), 0) // 2

    def group(turn, carry):
        field = [ref[pl.ds(64 * f + 8 * turn, 8), :] for f in range(9)]
        weight_x = kernel_weights(field[3])
        weight_y = kernel_weights(field[4])
        weight_z = kernel_weights(field[5])
        cell_x = field[6].astype(jnp.int32) + (7 + shift)
        cell_y = field[7].astype(jnp.int32) + 3
        cell_z = field[8].astype(jnp.int32) + 7
        low = [bounds_ref[number, 0, 4 * turn + k] + 7 for k in range(4)]
        high = [bounds_ref[number, 1, 4 * turn + k] + 10 for k in range(4)]
        turns = functools.reduce(
            jnp.maximum, [(high[k] - low[k] + WINDOW) // WINDOW for k in range(4)]
        )

        def window(step, inner):
            bases = [jnp.minimum(low[k] + step * WINDOW, DEPTH - 5) for k in range(4)]
            origin = jnp.full((8, 128), bases[0], jnp.int32)
            for k in range(1, 4):
                origin = jnp.where(owner == k, bases[k], origin)
            origin = origin - cell_z
            tall = [choose(origin + j, weight_z) for j in range(WINDOW)]
            for k in range(4):
                leads, crosses = [], []
                for half in (2 * k, 2 * k + 1):
                    row = slice(half, half + 1)
                    spread_x = choose(rows_x - cell_x[row], [w[row] for w in weight_x])
                    spread_y = choose(rows_y - cell_y[row], [w[row] for w in weight_y])
                    leads.append(
                        jnp.concatenate(
                            [
                                part
                                for c in range(3)
                                for part in (
                                    below, (field[c][row] * spread_x).astype(jnp.bfloat16), above
                                )
                                if part.shape[0]
                            ]
                            + [jnp.zeros((16, 128), jnp.bfloat16)],
                            0,
                        )
                    )
                    crosses.append(
                        jnp.concatenate(
                            [
                                jnp.concatenate(
                                    [tall[j][row] * spread_y, tall[j + 1][row] * spread_y], 0
                                ).astype(jnp.bfloat16)
                                for j in range(0, WINDOW, 2)
                            ],
                            0,
                        )
                    )
                product = lax.dot_general(
                    jnp.concatenate(crosses, 1), jnp.concatenate(leads, 1),
                    (((1,), (1,)), ((), ())), preferred_element_type=jnp.float32,
                )
                for j in range(WINDOW):
                    for half in range(2):
                        grid_ref[bases[k] + j, half] += product[
                            PLANES * j : PLANES * j + PLANES, 128 * half : 128 * half + 128
                        ]
            return inner

        lax.fori_loop(0, turns, window, 0)
        return carry

    lax.fori_loop(0, 8, group, 0)


def deposit_kernel(
    bounds_ref, side_ref, own_ref, low_ref, high_ref, brick_ref, near_ref, up_ref, down_ref,
    grid_ref, done,
):
    def clear(layer, carry):
        grid_ref[layer] = jnp.zeros((2, PLANES, 128), jnp.float32)
        return carry

    lax.fori_loop(0, LAYERS, clear, 0)
    add_source(bounds_ref, 0, own_ref, 0, grid_ref)
    add_source(bounds_ref, 1, low_ref, -64, grid_ref)
    add_source(bounds_ref, 2, high_ref, 64, grid_ref)
    copy = pltpu.make_async_copy(grid_ref.at[pl.ds(8, 128)], brick_ref, done)
    copy.start()
    flat_ref = grid_ref.reshape(2 * LAYERS * PLANES, 128)
    inner = jnp.where(side_ref[0] == 0, 132, 4)
    for layer in range(8):
        for half in range(2):
            start = PLANES * (2 * layer + half)
            near_ref[start : start + PLANES] = grid_ref[inner + layer, half]
    for target, plane in ((up_ref, 32), (down_ref, 1)):
        for k in range(7):
            for half in range(2):
                start = 256 * k + 128 * half
                target[start : start + 128] = flat_ref[
                    pl.ds((16 + half) * PLANES + plane + k, 128, stride=2 * PLANES), :
                ]
    copy.wait()


def deposit(bounds, side, own, low, high):
    vmem = pl.BlockSpec(memory_space=pltpu.VMEM)
    smem = pl.BlockSpec(memory_space=pltpu.SMEM)
    return pl.pallas_call(
        deposit_kernel,
        out_shape=(
            jax.ShapeDtypeStruct((128, 2, PLANES, 128), jnp.float32),
            jax.ShapeDtypeStruct((16 * PLANES, 128), jnp.float32),
            jax.ShapeDtypeStruct((1792, 128), jnp.float32),
            jax.ShapeDtypeStruct((1792, 128), jnp.float32),
        ),
        in_specs=[smem, smem, vmem, vmem, vmem],
        out_specs=(pl.BlockSpec(memory_space=pltpu.HBM),) + (vmem,) * 3,
        scratch_shapes=[
            pltpu.VMEM((LAYERS, 2, PLANES, 128), jnp.float32),
            pltpu.SemaphoreType.DMA(()),
        ],
        compiler_params=pltpu.CompilerParams(vmem_limit_bytes=24 * 1024 * 1024),
        cost_estimate=pl.CostEstimate(
            flops=16_000_000_000, bytes_accessed=40_000_000, transcendentals=0
        ),
        name="deposit",
    )(bounds, side, own, low, high)


def faces_kernel(
    up_own_ref, down_own_ref, near_ref, swapped_ref, first_ref, last_ref, slab_ref, slab_other_ref,
    up_ref, down_ref,
):
    for target, own, plane, other, speed_ref, skip in (
        (up_ref, up_own_ref, 32, 28, last_ref, 3), (down_ref, down_own_ref, 1, 0, first_ref, 0)
    ):
        for k in range(7):
            for half in range(2):
                start = 272 * k + 136 * half
                first = PLANES * half + plane + k
                block = 256 * k + 128 * half
                target[start : start + 128] = own[block : block + 128]
                target[start + 128 : start + 136] = (
                    near_ref[pl.ds(first, 8, stride=2 * PLANES), :]
                    + swapped_ref[pl.ds(first, 8, stride=2 * PLANES), :]
                )
        for k in range(4):
            target[1904 + 240 * k : 2144 + 240 * k] = speed_ref[skip + k]
            for half in range(2):
                start = 2864 + 16 * k + 8 * half
                target[start : start + 8] = (
                    slab_ref[other + k, half] + slab_other_ref[other + k, half]
                )


def faces(*arrays):
    vmem = pl.BlockSpec(memory_space=pltpu.VMEM)
    return pl.pallas_call(
        faces_kernel,
        out_shape=(jax.ShapeDtypeStruct((2928, 128), jnp.float32),) * 2,
        in_specs=[vmem] * 8,
        out_specs=(vmem, vmem),
        compiler_params=pltpu.CompilerParams(vmem_limit_bytes=24 * 1024 * 1024),
        name="faces",
    )(*arrays)


def cut_kernel(main_ref, up_ref, down_ref, done):
    copies = []
    for c in range(3):
        for k, (target, start) in enumerate(((up_ref, 1920), (down_ref, 0))):
            copies.append(
                pltpu.make_async_copy(
                    main_ref.at[pl.ds(2048 * c + start, 128)],
                    target.at[pl.ds(128 * c, 128)],
                    done.at[2 * c + k],
                )
            )
    for copy in copies:
        copy.start()
    for copy in copies:
        copy.wait()


def cut_velocity(main):
    vmem = pl.BlockSpec(memory_space=pltpu.VMEM)
    return pl.pallas_call(
        cut_kernel,
        out_shape=(jax.ShapeDtypeStruct((384, 128), jnp.float32),) * 2,
        in_specs=[pl.BlockSpec(memory_space=pl.ANY)],
        out_specs=(vmem, vmem),
        scratch_shapes=[pltpu.SemaphoreType.DMA((6,))],
        name="cut_velocity",
    )(main)


def velocity_rows(main_ref, low_ref, high_ref, y, c):
    blank = jnp.zeros((4, 128), jnp.float32)
    return jnp.concatenate(
        [
            blank,
            low_ref[pl.ds(128 * c + y, 4, stride=32), :],
            main_ref[pl.ds(2048 * c + y, 64, stride=32), :],
            high_ref[pl.ds(128 * c + y, 4, stride=32), :],
            blank,
        ],
        0,
    )


def velocity_kernel(
    side_ref, main_ref, low_ref, high_ref, slab_ref, first_ref, last_ref, gather_ref
):
    upper = side_ref[0] == 0
    lane = lax.broadcasted_iota(jnp.int32, (GROUP, 128), 1)
    target = jnp.where(upper, 0, 4)
    gather_ref[ROWS:256] = jnp.zeros((256 - ROWS, 128), jnp.float32)

    def sixteen(turn, carry):
        for c in range(3):
            gathered = jnp.zeros((GROUP, 128), jnp.float32)
            for k in range(16):
                rows = velocity_rows(main_ref, low_ref, high_ref, 16 * turn + k, c)
                moved = pltpu.roll(rows, (8 * k + 4) % 128, 1)
                goal = 8 * k + target
                gathered = jnp.where((lane >= goal) & (lane < goal + 4), moved, gathered)
            gather_ref[GROUP * c : GROUP * c + GROUP] = gathered
        slabs = jnp.transpose(gather_ref[...])
        for half in range(2):
            slab_ref[pl.ds(16 * turn, 16), half] = slabs[
                :, 128 * half : 128 * half + 128
            ].reshape(16, 8, 128)
        return carry

    lax.fori_loop(0, 2, sixteen, 0)
    for k in range(7):
        for c in range(3):
            rows = slice(GROUP * c, GROUP * c + GROUP)
            first_ref[k, rows] = velocity_rows(main_ref, low_ref, high_ref, k, c)
            last_ref[k, rows] = velocity_rows(main_ref, low_ref, high_ref, 25 + k, c)


def arrange_velocity(side, main, low, high):
    vmem = pl.BlockSpec(memory_space=pltpu.VMEM)
    smem = pl.BlockSpec(memory_space=pltpu.SMEM)
    return pl.pallas_call(
        velocity_kernel,
        out_shape=(
            jax.ShapeDtypeStruct((32, 2, 8, 128), jnp.float32),
            jax.ShapeDtypeStruct((7, ROWS, 128), jnp.float32),
            jax.ShapeDtypeStruct((7, ROWS, 128), jnp.float32),
        ),
        in_specs=[smem, vmem, vmem, vmem],
        out_specs=(vmem, vmem, vmem),
        scratch_shapes=[pltpu.VMEM((256, 128), jnp.float32)],
        compiler_params=pltpu.CompilerParams(vmem_limit_bytes=16 * 1024 * 1024),
        cost_estimate=pl.CostEstimate(
            flops=4_000_000_000, bytes_accessed=8_000_000, transcendentals=0
        ),
        name="arrange_velocity",
    )(side, main, low, high)


def bands(upper, odd):
    source = lax.broadcasted_iota(jnp.int32, (128, 128), 0)
    target = lax.broadcasted_iota(jnp.int32, (128, 128), 1)

    def entries(distance):
        near = jnp.where(distance == 1, 8.0 if odd else 16.0, 0.0)
        near = jnp.where(distance == -1, -8.0 if odd else 16.0, near)
        near = jnp.where(distance == 2, -1.0, near)
        return jnp.where(distance == -2, 1.0 if odd else -1.0, near)

    main = entries(source - target).astype(jnp.bfloat16)
    layer = source % 8
    begin = jnp.where(upper, 4, 0)
    outer = (layer >= begin) & (layer < begin + 4)
    halo = jnp.where(outer, entries(layer + jnp.where(upper, 124, -4) - target), 0.0)
    return main, halo, source // 8


SCALE_L = 0.1 * 0.5 / 12.0
SCALE_D = 0.1 / 12.0


def fill_bands(upper, even_ref, odd_ref):
    for odd, ref in ((False, even_ref), (True, odd_ref)):
        main, halo, owner = bands(upper, odd)
        for k in range(16):
            ref[k, 0:128] = main
            ref[k, 128:256] = jnp.where(owner == k, halo, 0.0).astype(jnp.bfloat16)


def row_mask(place_ref):
    row = lax.broadcasted_iota(jnp.int32, (GROUP, 128), 0)
    start = jnp.where(place_ref[0] == 0, 8, 0)
    stop = jnp.where(place_ref[0] == place_ref[1] - 1, 72, GROUP)
    return jnp.where((row >= start) & (row < stop), 1.0, 0.0)


def lane_mask(place_ref):
    lane = lax.broadcasted_iota(jnp.int32, (8, 256), 1)
    column = lane % GROUP
    start = jnp.where(place_ref[0] == 0, 8, 0)
    stop = jnp.where(place_ref[0] == place_ref[1] - 1, 72, GROUP)
    mask = jnp.where((column >= start) & (column < stop), 1.0, 0.0)
    return jnp.where(lane < ROWS, mask, 0.0)


def own_slab(near_ref, swapped_ref, plane):
    return jnp.concatenate(
        [
            near_ref[pl.ds(half * PLANES + plane, 8, stride=2 * PLANES), :]
            + swapped_ref[pl.ds(half * PLANES + plane, 8, stride=2 * PLANES), :]
            for half in range(2)
        ],
        1,
    )


def place_mesh(w_ref, a_ref, index, plane, main, slab, upper, inside, inside_slab):
    layer = lax.broadcasted_iota(jnp.int32, (8, 256), 0)
    slab = slab * inside_slab
    a_ref[plane] = slab
    inner = pltpu.roll(slab, 4, 0)
    bottom = jnp.where((layer < 4) & (layer < jnp.where(upper, 0, 8)), inner, main[0:8])
    top = jnp.where((layer >= 4) & (layer < jnp.where(upper, 8, 0)), inner, main[120:128])
    turned = jnp.transpose(jnp.concatenate([bottom, main[8:120], top], 0))
    zeros = jnp.zeros((8, 128), jnp.float32)
    w_ref[index, 0:8] = zeros
    w_ref[index, 248:256] = zeros
    for c in range(3):
        rows = slice(GROUP * c, GROUP * c + GROUP)
        w_ref[index, 8 + GROUP * c : 88 + GROUP * c] = turned[rows] * inside


def place_speed(v_ref, index, main):
    zeros = jnp.zeros((8, 128), jnp.float32)
    v_ref[index, 0:8] = zeros
    v_ref[index, 248:256] = zeros
    v_ref[index, 8:248] = main


def turn_slabs(source_ref, target_ref, groups):
    for g in range(groups):
        stacked = jnp.concatenate([source_ref[16 * g + k] for k in range(16)], 0)
        target_ref[g] = jnp.transpose(stacked)[:ROWS].astype(jnp.bfloat16)


def along_z(main, halo, matrix):
    return jnp.dot(
        jnp.concatenate([main.astype(jnp.bfloat16), halo], 1), matrix,
        preferred_element_type=jnp.float32,
    )


def part(ref, index, c, dx):
    start = 8 + GROUP * c + dx
    return ref[index, start : start + GROUP]


def curvature(ref, at, c):
    near = part(ref, at(1), c, 0) + part(ref, at(-1), c, 0) + (
        part(ref, at(0), c, 1) + part(ref, at(0), c, -1)
    )
    far = part(ref, at(2), c, 0) + part(ref, at(-2), c, 0) + (
        part(ref, at(0), c, 2) + part(ref, at(0), c, -2)
    )
    return 16.0 * near - far


def first_plane(w_ref, w_at, v_ref, v_at, curve, climb, c, centre):
    rows = slice(GROUP * c, GROUP * c + GROUP)
    here = v_at(0)
    slope_x = 8.0 * (part(v_ref, here, c, 1) - part(v_ref, here, c, -1)) - (
        part(v_ref, here, c, 2) - part(v_ref, here, c, -2)
    )
    slope_y = 8.0 * (part(v_ref, v_at(1), c, 0) - part(v_ref, v_at(-1), c, 0)) - (
        part(v_ref, v_at(2), c, 0) - part(v_ref, v_at(-2), c, 0)
    )
    slopes = (slope_x, slope_y, climb[rows])
    stretch = centre[0] * slopes[0] + centre[1] * slopes[1] + centre[2] * slopes[2]
    result = (
        centre[c] * (1.0 - 90.0 * SCALE_L)
        + SCALE_L * (curvature(w_ref, w_at, c) + curve[rows])
        + SCALE_D * stretch
    )
    return result, slopes


def interior_kernel(
    place_ref, grid_ref, near_ref, swapped_ref, main_ref, behind_ref, ahead_ref, slab_ref, slab_other_ref,
    f_out_ref, d_out_ref, w_edge_ref,
    w_ref, wt_ref, a_ref, v_ref, vt_ref, b_ref, even_ref, odd_ref, f_ref, d_ref, done,
):
    upper = place_ref[4] == 0
    inside = row_mask(place_ref)
    inside_slab = lane_mask(place_ref)
    fill_bands(upper, even_ref, odd_ref)

    def mesh_plane(plane, carry):
        main = jnp.concatenate(
            [
                grid_ref[pl.ds(half * PLANES + plane, 128, stride=2 * PLANES), :]
                for half in range(2)
            ],
            1,
        )
        slab = own_slab(near_ref, swapped_ref, plane)
        place_mesh(w_ref, a_ref, plane - 7, plane, main, slab, upper, inside, inside_slab)
        return carry

    blank = jnp.zeros((8, 256), jnp.float32)
    for plane in tuple(range(7)) + tuple(range(33, 48)):
        a_ref[plane] = blank
    for plane in tuple(range(4)) + tuple(range(36, 48)):
        b_ref[plane] = blank
    lax.fori_loop(7, 33, mesh_plane, 0, unroll=2)

    def speed_plane(plane, carry):
        place_speed(
            v_ref, plane,
            jnp.concatenate(
                [velocity_rows(main_ref, behind_ref, ahead_ref, plane, c) for c in range(3)], 0
            ),
        )
        slab = slab_ref[plane] + slab_other_ref[plane]
        b_ref[plane + 4] = jnp.concatenate([slab[0], slab[1]], 1)
        return carry

    lax.fori_loop(0, 32, speed_plane, 0)
    turn_slabs(a_ref, wt_ref, 2)
    turn_slabs(b_ref, vt_ref, 2)
    for k in range(4):
        w_edge_ref[k] = w_ref[k]
        w_edge_ref[4 + k] = w_ref[22 + k]

    def step(k, carry):
        y = k + 9
        curve = along_z(w_ref[y - 7, 8:248], wt_ref[y >> 4], even_ref[y & 15])
        climb = along_z(v_ref[y - 4, 8:248], vt_ref[y >> 4], odd_ref[y & 15])
        zeros = jnp.zeros((8, 128), jnp.float32)
        f_ref[k, 0:8] = zeros
        f_ref[k, 248:256] = zeros
        centre = [part(w_ref, y - 7, c, 0) for c in range(3)]
        for c in range(3):
            result, slopes = first_plane(
                w_ref, lambda o: y - 7 + o, v_ref, lambda o: y - 4 + o, curve, climb, c, centre
            )
            for d in range(3):
                d_ref[k, d, GROUP * c : GROUP * c + GROUP] = slopes[d].astype(jnp.bfloat16)
            f_ref[k, 8 + GROUP * c : 88 + GROUP * c] = result * inside
        return carry

    lax.fori_loop(0, 22, step, 0, unroll=2)
    copies = [
        pltpu.make_async_copy(f_ref, f_out_ref, done.at[0]),
        pltpu.make_async_copy(d_ref, d_out_ref, done.at[1]),
    ]
    for copy in copies:
        copy.start()
    for copy in copies:
        copy.wait()


def interior(*arrays):
    vmem = pl.BlockSpec(memory_space=pltpu.VMEM)
    smem = pl.BlockSpec(memory_space=pltpu.SMEM)
    scratch = [
        pltpu.VMEM((26, 256, 128), jnp.float32),
        pltpu.VMEM((2, ROWS, 128), jnp.bfloat16),
        pltpu.VMEM((48, 8, 256), jnp.float32),
        pltpu.VMEM((32, 256, 128), jnp.float32),
        pltpu.VMEM((2, ROWS, 128), jnp.bfloat16),
        pltpu.VMEM((48, 8, 256), jnp.float32),
        pltpu.VMEM((16, 256, 128), jnp.bfloat16),
        pltpu.VMEM((16, 256, 128), jnp.bfloat16),
        pltpu.VMEM((22, 256, 128), jnp.float32),
        pltpu.VMEM((22, 3, ROWS, 128), jnp.bfloat16),
        pltpu.SemaphoreType.DMA((2,)),
    ]
    hbm = pl.BlockSpec(memory_space=pltpu.HBM)
    return pl.pallas_call(
        interior_kernel,
        out_shape=(
            jax.ShapeDtypeStruct((22, 256, 128), jnp.float32),
            jax.ShapeDtypeStruct((22, 3, ROWS, 128), jnp.bfloat16),
            jax.ShapeDtypeStruct((8, 256, 128), jnp.float32),
        ),
        in_specs=[smem] + [vmem] * 8,
        out_specs=(hbm, hbm, vmem),
        scratch_shapes=scratch,
        compiler_params=pltpu.CompilerParams(vmem_limit_bytes=34 * 1024 * 1024),
        cost_estimate=pl.CostEstimate(
            flops=15_000_000_000, bytes_accessed=40_000_000, transcendentals=0
        ),
        name="interior",
    )(*arrays)


def edges_kernel(
    place_ref, f_in_ref, d_in_ref, w_edge_ref, speed_low_ref, speed_high_ref,
    near_ref, swapped_ref, slab_ref, slab_other_ref, own_high_ref, own_low_ref, low_ref, high_ref,
    out_ref, w_ref, wt_ref, a_ref, v_ref, vt_ref, b_ref, f_ref, e_ref, even_ref, odd_ref, d_ref, d_mid_ref, done,
):
    copies = [
        pltpu.make_async_copy(f_in_ref, f_ref.at[pl.ds(7, 22)], done.at[0]),
        pltpu.make_async_copy(d_in_ref, d_mid_ref, done.at[1]),
    ]
    for copy in copies:
        copy.start()
    upper = place_ref[4] == 0
    inside = row_mask(place_ref)
    inside_slab = lane_mask(place_ref)
    keep_low = jnp.where(place_ref[2] == 0, 0.0, 1.0)
    keep_high = jnp.where(place_ref[2] == place_ref[3] - 1, 0.0, 1.0)
    fill_bands(upper, even_ref, odd_ref)

    def block(ref, k, start, stop):
        base = 272 * k
        return jnp.concatenate(
            [ref[base + start : base + stop], ref[base + 136 + start : base + 136 + stop]], 1
        )

    for plane in range(7):
        for ref, own_ref, k, own_k, at, keep in (
            (low_ref, own_low_ref, plane, plane - 1, plane, keep_low if plane < 4 else None),
            (high_ref, own_high_ref, plane, plane + 1, plane + 33, keep_high if plane >= 3 else None),
        ):
            main, slab = block(ref, k, 0, 128), block(ref, k, 128, 136)
            if 0 <= own_k < 7:
                main, slab = main + block(own_ref, own_k, 0, 128), slab + block(own_ref, own_k, 128, 136)
            else:
                slab = slab + own_slab(near_ref, swapped_ref, at)
            if keep is not None:
                main, slab = main * keep, slab * keep
            index = at if at < 20 else at - 18
            place_mesh(w_ref, a_ref, index, at, main, slab, upper, inside, inside_slab)
    for k in range(4):
        w_ref[7 + k] = w_edge_ref[k]
        w_ref[11 + k] = w_edge_ref[4 + k]

    def middle_slab(plane, carry):
        a_ref[plane] = own_slab(near_ref, swapped_ref, plane) * inside_slab
        return carry

    lax.fori_loop(7, 33, middle_slab, 0, unroll=2)
    for ref, begin, index in ((low_ref, 0, 0), (high_ref, 36, 18)):
        for k in range(4):
            start, end = 1904 + 240 * k, 2864 + 16 * k
            place_speed(v_ref, index + k, ref[start : start + 240])
            b_ref[begin + k] = jnp.concatenate([ref[end : end + 8], ref[end + 8 : end + 16]], 1)
    for k in range(7):
        place_speed(v_ref, 4 + k, speed_low_ref[k])
        place_speed(v_ref, 11 + k, speed_high_ref[k])

    def speed_slab(plane, carry):
        slab = slab_ref[plane] + slab_other_ref[plane]
        b_ref[plane + 4] = jnp.concatenate([slab[0], slab[1]], 1)
        return carry

    lax.fori_loop(0, 32, speed_slab, 0, unroll=4)
    blank = jnp.zeros((8, 256), jnp.float32)
    for k in range(40, 48):
        a_ref[k] = blank
        b_ref[k] = blank
    turn_slabs(a_ref, wt_ref, 3)
    turn_slabs(b_ref, vt_ref, 3)

    for copy in copies:
        copy.wait()

    def first_steps(start, lag, lag_f, lag_d, keep, outside, stored):
        def step(k, carry):
            y = k + start
            curve = along_z(w_ref[y - lag, 8:248], wt_ref[y >> 4], even_ref[y & 15])
            climb = along_z(v_ref[y - lag, 8:248], vt_ref[y >> 4], odd_ref[y & 15])
            zeros = jnp.zeros((8, 128), jnp.float32)
            scale = jnp.where((k >= outside[0]) & (k < outside[1]), keep, 1.0)
            f_ref[y - lag_f, 0:8] = zeros
            f_ref[y - lag_f, 248:256] = zeros
            centre = [part(w_ref, y - lag, c, 0) for c in range(3)]
            at = lambda o: y - lag + o
            for c in range(3):
                result, slopes = first_plane(w_ref, at, v_ref, at, curve, climb, c, centre)
                for d in range(3):
                    d_ref[y - lag_d, d, GROUP * c : GROUP * c + GROUP] = slopes[d].astype(jnp.bfloat16)
                f_ref[y - lag_f, 8 + GROUP * c : 88 + GROUP * c] = result * (inside * scale)
            return carry

        lax.fori_loop(0, 7, step, 0, unroll=stored)

    first_steps(2, 0, 2, 2, keep_low, (0, 2), 1)
    first_steps(31, 18, 2, 24, keep_high, (5, 7), 1)

    lane = lax.broadcasted_iota(jnp.int32, (8, 256), 1)
    group = lane // GROUP

    def slab_step(k, carry):
        y = k + 4
        here = a_ref[y]
        speed = b_ref[y]

        def both_ways(array, step, axis):
            size = array.shape[axis]
            return pltpu.roll(array, size - step, axis), pltpu.roll(array, step, axis)

        ax1, bx1 = both_ways(here, 1, 1)
        ax2, bx2 = both_ways(here, 2, 1)
        az1, bz1 = both_ways(here, 1, 0)
        az2, bz2 = both_ways(here, 2, 0)
        near = a_ref[y + 1] + a_ref[y - 1] + (ax1 + bx1) + (az1 + bz1)
        far = a_ref[y + 2] + a_ref[y - 2] + (ax2 + bx2) + (az2 + bz2)
        vx1, ux1 = both_ways(speed, 1, 1)
        vx2, ux2 = both_ways(speed, 2, 1)
        vz1, uz1 = both_ways(speed, 1, 0)
        vz2, uz2 = both_ways(speed, 2, 0)
        slope_x = 8.0 * (vx1 - ux1) - (vx2 - ux2)
        slope_y = 8.0 * (b_ref[y + 1] - b_ref[y - 1]) - (b_ref[y + 2] - b_ref[y - 2])
        slope_z = 8.0 * (vz1 - uz1) - (vz2 - uz2)
        right1 = pltpu.roll(here, GROUP, 1)
        right2 = pltpu.roll(here, 2 * GROUP, 1)
        left1 = pltpu.roll(here, 256 - GROUP, 1)
        left2 = pltpu.roll(here, 256 - 2 * GROUP, 1)
        swirl_x = jnp.where(group == 0, here, jnp.where(group == 1, right1, right2))
        swirl_y = jnp.where(group == 0, left1, jnp.where(group == 1, here, right1))
        swirl_z = jnp.where(group == 0, left2, jnp.where(group == 1, left1, here))
        e_ref[k] = (
            here * (1.0 - 90.0 * SCALE_L)
            + SCALE_L * (16.0 * near - far)
            + SCALE_D * (swirl_x * slope_x + swirl_y * slope_y + swirl_z * slope_z)
        )
        return carry

    lax.fori_loop(0, 32, slab_step, 0, unroll=2)
    turn_slabs(e_ref, vt_ref, 2)

    def second(slopes_ref, index, k):
        y = k + 2
        curve = along_z(f_ref[y, 8:248], vt_ref[k >> 4], even_ref[k & 15])
        centre = [part(f_ref, y, c, 0) for c in range(3)]
        for c in range(3):
            rows = slice(GROUP * c, GROUP * c + GROUP)
            slopes = [slopes_ref[index, d, rows].astype(jnp.float32) for d in range(3)]
            stretch = centre[0] * slopes[0] + centre[1] * slopes[1] + centre[2] * slopes[2]
            result = (
                centre[c] * (1.0 - 90.0 * SCALE_L)
                + SCALE_L * (curvature(f_ref, lambda o: y + o, c) + curve[rows])
                + SCALE_D * stretch
            )
            out_ref[pl.ds(2048 * c + k, 64, stride=32), :] = result[8:72]

    def second_low(k, carry):
        second(d_ref, k + 2, k)
        return carry

    def second_high(k, carry):
        second(d_ref, k - 20, k)
        return carry

    def second_middle(k, carry):
        second(d_mid_ref, k - 5, k)
        return carry

    lax.fori_loop(0, 5, second_low, 0)
    lax.fori_loop(27, 32, second_high, 0)
    lax.fori_loop(5, 27, second_middle, 0, unroll=2)


def edges(*arrays):
    vmem = pl.BlockSpec(memory_space=pltpu.VMEM)
    smem = pl.BlockSpec(memory_space=pltpu.SMEM)
    scratch = [
        pltpu.VMEM((22, 256, 128), jnp.float32),
        pltpu.VMEM((3, ROWS, 128), jnp.bfloat16),
        pltpu.VMEM((48, 8, 256), jnp.float32),
        pltpu.VMEM((22, 256, 128), jnp.float32),
        pltpu.VMEM((3, ROWS, 128), jnp.bfloat16),
        pltpu.VMEM((48, 8, 256), jnp.float32),
        pltpu.VMEM((36, 256, 128), jnp.float32),
        pltpu.VMEM((32, 8, 256), jnp.float32),
        pltpu.VMEM((16, 256, 128), jnp.bfloat16),
        pltpu.VMEM((16, 256, 128), jnp.bfloat16),
        pltpu.VMEM((14, 3, ROWS, 128), jnp.bfloat16),
        pltpu.VMEM((22, 3, ROWS, 128), jnp.bfloat16),
        pltpu.SemaphoreType.DMA((2,)),
    ]
    hbm = pl.BlockSpec(memory_space=pltpu.HBM)
    return pl.pallas_call(
        edges_kernel,
        out_shape=jax.ShapeDtypeStruct((3 * 64 * 32, 128), jnp.float32),
        in_specs=[smem, hbm, hbm] + [vmem] * 11,
        out_specs=vmem,
        scratch_shapes=scratch,
        compiler_params=pltpu.CompilerParams(vmem_limit_bytes=38 * 1024 * 1024),
        name="edges",
    )(*arrays)


def sort_inputs(strength, fraction, stream_cell, span_cell, height_cell):
    key = ((height_cell + 2) << 16) | ((stream_cell + 2) << 8) | (span_cell + 2)
    load = strength.astype(jnp.float32)
    return lax.sort(
        (key, load[0], load[1], load[2], fraction[0], fraction[1], fraction[2]),
        num_keys=1, is_stable=False,
    )


def pack_kernel(key_ref, *refs):
    fields, packed_ref = refs[:6], refs[6]
    key = key_ref[...]
    cells = ((key >> 8) & 255, key & 255, key >> 16)
    for f in range(6):
        packed_ref[64 * f : 64 * f + 64] = fields[f][...]
    for f in range(3):
        packed_ref[384 + 64 * f : 448 + 64 * f] = (cells[f] - 2).astype(jnp.float32)


def pack(parts):
    vmem = pl.BlockSpec(memory_space=pltpu.VMEM)
    return pl.pallas_call(
        pack_kernel,
        out_shape=jax.ShapeDtypeStruct((576, 128), jnp.float32),
        in_specs=[vmem] * 7,
        out_specs=vmem,
        compiler_params=pltpu.CompilerParams(vmem_limit_bytes=16 * 1024 * 1024),
        name="pack",
    )(*[p.reshape(64, 128) for p in parts])


def shards(strength, fraction, stream_cell, span_cell, height_cell, velocity):
    count_x, count_y = lax.axis_size("gx"), lax.axis_size("gy")
    index_x, index_y, index_z = (lax.axis_index(a) for a in ("gx", "gy", "gz"))
    side = index_z.astype(jnp.int32).reshape(1)
    place = jnp.stack(
        [index_x, jnp.int32(count_x), index_y, jnp.int32(count_y), index_z]
    ).astype(jnp.int32)
    up_x = [(i, i + 1) for i in range(count_x - 1)]
    down_x = [(j, i) for i, j in up_x]
    up_y = [(i, i + 1) for i in range(count_y - 1)]
    velocity = velocity.reshape(6144, 128)
    upward, downward = cut_velocity(velocity)
    low_speed = lax.ppermute(upward, "gx", up_x)
    high_speed = lax.ppermute(downward, "gx", down_x)
    parts = sort_inputs(strength, fraction, stream_cell, span_cell, height_cell)
    packed = pack(parts)
    low = lax.ppermute(packed, "gx", up_x)
    high = lax.ppermute(packed, "gx", down_x)

    def limits(block):
        span = block[512:576].reshape(32, 256)
        return jnp.stack([span[:, 0], span[:, 255]]).astype(jnp.int32)

    speed_slab, speed_first, speed_last = arrange_velocity(side, velocity, low_speed, high_speed)
    swap = [(0, 1), (1, 0)]
    other_slab = lax.ppermute(speed_slab, "gz", swap)
    bounds = jnp.stack([limits(packed), limits(low), limits(high)])
    grid, near, up_mesh, down_mesh = deposit(bounds, side, packed, low, high)
    swapped = lax.ppermute(near, "gz", swap)
    to_high, to_low = faces(
        up_mesh, down_mesh, near, swapped, speed_first, speed_last, speed_slab, other_slab
    )
    from_low = lax.ppermute(to_high, "gy", up_y)
    from_high = lax.ppermute(to_low, "gy", [(j, i) for i, j in up_y])
    grid = grid.reshape(256 * PLANES, 128)
    middle, slopes, mesh_edges = interior(
        place, grid, near, swapped, velocity, low_speed, high_speed, speed_slab, other_slab
    )
    out = edges(
        place, middle, slopes, mesh_edges, speed_first, speed_last, near, swapped,
        speed_slab, other_slab, to_high, to_low, from_low, from_high,
    )
    return out.reshape(3, 64, 32, 128)


def solution(mesh):
    return jax.shard_map(
        shards,
        mesh=mesh,
        in_specs=(
            P(None, ("gx", "gy", "gz")),
            P(None, ("gx", "gy", "gz")),
            P(("gx", "gy", "gz")),
            P(("gx", "gy", "gz")),
            P(("gx", "gy", "gz")),
            P(None, "gx", "gy", "gz"),
        ),
        out_specs=P(None, "gx", "gy", "gz"),
        check_vma=False,
    )
```

```python
import functools

import jax
import jax.numpy as jnp
from jax import lax
from jax.experimental import pallas as pl
from jax.experimental.pallas import tpu as pltpu
from jax.sharding import PartitionSpec as P

GROUP = 80
ROWS = 240
PLANES = 40
DEPTH = 144
WINDOW = 10
LAYERS = DEPTH + 5


def kernel_weights(fraction):
    remainder = 1.0 - fraction
    return (
        -0.5 * fraction * remainder * remainder,
        1.0 - 2.5 * fraction * fraction + 1.5 * fraction * fraction * fraction,
        1.0 - 2.5 * remainder * remainder + 1.5 * remainder * remainder * remainder,
        -0.5 * fraction * fraction * remainder,
    )


def choose(distance, weights):
    total = jnp.where(distance == 3, weights[3], 0.0)
    for offset in (2, 1, 0):
        total = jnp.where(distance == offset, weights[offset], total)
    return total


def add_source(bounds_ref, number, ref, shift, grid_ref):
    start_x, count_x = {0: (0, GROUP), -64: (0, 16), 64: (64, 16)}[shift]
    rows_x = lax.broadcasted_iota(jnp.int32, (count_x, 128), 0) + start_x
    below = jnp.zeros((start_x, 128), jnp.bfloat16)
    above = jnp.zeros((GROUP - start_x - count_x, 128), jnp.bfloat16)
    rows_y = lax.broadcasted_iota(jnp.int32, (PLANES, 128), 0)
    owner = lax.broadcasted_iota(jnp.int32, (8, 128), 0) // 2

    def group(turn, carry):
        field = [ref[pl.ds(64 * f + 8 * turn, 8), :] for f in range(9)]
        weight_x = kernel_weights(field[3])
        weight_y = kernel_weights(field[4])
        weight_z = kernel_weights(field[5])
        cell_x = field[6].astype(jnp.int32) + (7 + shift)
        cell_y = field[7].astype(jnp.int32) + 3
        cell_z = field[8].astype(jnp.int32) + 7
        low = [bounds_ref[number, 0, 4 * turn + k] + 7 for k in range(4)]
        high = [bounds_ref[number, 1, 4 * turn + k] + 10 for k in range(4)]
        turns = functools.reduce(
            jnp.maximum, [(high[k] - low[k] + WINDOW) // WINDOW for k in range(4)]
        )

        def window(step, inner):
            bases = [jnp.minimum(low[k] + step * WINDOW, DEPTH - 5) for k in range(4)]
            origin = jnp.full((8, 128), bases[0], jnp.int32)
            for k in range(1, 4):
                origin = jnp.where(owner == k, bases[k], origin)
            origin = origin - cell_z
            tall = [choose(origin + j, weight_z) for j in range(WINDOW)]
            for k in range(4):
                leads, crosses = [], []
                for half in (2 * k, 2 * k + 1):
                    row = slice(half, half + 1)
                    spread_x = choose(rows_x - cell_x[row], [w[row] for w in weight_x])
                    spread_y = choose(rows_y - cell_y[row], [w[row] for w in weight_y])
                    leads.append(
                        jnp.concatenate(
                            [
                                part
                                for c in range(3)
                                for part in (
                                    below, (field[c][row] * spread_x).astype(jnp.bfloat16), above
                                )
                                if part.shape[0]
                            ]
                            + [jnp.zeros((16, 128), jnp.bfloat16)],
                            0,
                        )
                    )
                    crosses.append(
                        jnp.concatenate(
                            [
                                jnp.concatenate(
                                    [tall[j][row] * spread_y, tall[j + 1][row] * spread_y], 0
                                ).astype(jnp.bfloat16)
                                for j in range(0, WINDOW, 2)
                            ],
                            0,
                        )
                    )
                product = lax.dot_general(
                    jnp.concatenate(crosses, 1), jnp.concatenate(leads, 1),
                    (((1,), (1,)), ((), ())), preferred_element_type=jnp.float32,
                )
                for j in range(WINDOW):
                    for half in range(2):
                        grid_ref[bases[k] + j, half] += product[
                            PLANES * j : PLANES * j + PLANES, 128 * half : 128 * half + 128
                        ]
            return inner

        lax.fori_loop(0, turns, window, 0)
        return carry

    lax.fori_loop(0, 8, group, 0)


def deposit_kernel(
    bounds_ref, side_ref, own_ref, low_ref, high_ref, brick_ref, near_ref, up_ref, down_ref,
    grid_ref, done,
):
    def clear(layer, carry):
        grid_ref[layer] = jnp.zeros((2, PLANES, 128), jnp.float32)
        return carry

    lax.fori_loop(0, LAYERS, clear, 0)
    add_source(bounds_ref, 0, own_ref, 0, grid_ref)
    add_source(bounds_ref, 1, low_ref, -64, grid_ref)
    add_source(bounds_ref, 2, high_ref, 64, grid_ref)
    copy = pltpu.make_async_copy(grid_ref.at[pl.ds(8, 128)], brick_ref, done)
    copy.start()
    flat_ref = grid_ref.reshape(2 * LAYERS * PLANES, 128)
    inner = jnp.where(side_ref[0] == 0, 132, 4)
    for layer in range(8):
        for half in range(2):
            start = PLANES * (2 * layer + half)
            near_ref[start : start + PLANES] = grid_ref[inner + layer, half]
    for target, plane in ((up_ref, 32), (down_ref, 1)):
        for k in range(7):
            for half in range(2):
                start = 256 * k + 128 * half
                target[start : start + 128] = flat_ref[
                    pl.ds((16 + half) * PLANES + plane + k, 128, stride=2 * PLANES), :
                ]
    copy.wait()


def deposit(bounds, side, own, low, high):
    vmem = pl.BlockSpec(memory_space=pltpu.VMEM)
    smem = pl.BlockSpec(memory_space=pltpu.SMEM)
    return pl.pallas_call(
        deposit_kernel,
        out_shape=(
            jax.ShapeDtypeStruct((128, 2, PLANES, 128), jnp.float32),
            jax.ShapeDtypeStruct((16 * PLANES, 128), jnp.float32),
            jax.ShapeDtypeStruct((1792, 128), jnp.float32),
            jax.ShapeDtypeStruct((1792, 128), jnp.float32),
        ),
        in_specs=[smem, smem, vmem, vmem, vmem],
        out_specs=(pl.BlockSpec(memory_space=pl.ANY),) + (vmem,) * 3,
        scratch_shapes=[
            pltpu.VMEM((LAYERS, 2, PLANES, 128), jnp.float32),
            pltpu.SemaphoreType.DMA(()),
        ],
        compiler_params=pltpu.CompilerParams(vmem_limit_bytes=24 * 1024 * 1024),
        cost_estimate=pl.CostEstimate(
            flops=16_000_000_000, bytes_accessed=40_000_000, transcendentals=0
        ),
        name="deposit",
    )(bounds, side, own, low, high)


def faces_kernel(
    up_own_ref, down_own_ref, near_ref, swapped_ref, first_ref, last_ref, slab_ref, slab_other_ref,
    up_ref, down_ref,
):
    for target, own, plane, other, speed_ref, skip in (
        (up_ref, up_own_ref, 32, 28, last_ref, 3), (down_ref, down_own_ref, 1, 0, first_ref, 0)
    ):
        for k in range(7):
            for half in range(2):
                start = 272 * k + 136 * half
                first = PLANES * half + plane + k
                block = 256 * k + 128 * half
                target[start : start + 128] = own[block : block + 128]
                target[start + 128 : start + 136] = (
                    near_ref[pl.ds(first, 8, stride=2 * PLANES), :]
                    + swapped_ref[pl.ds(first, 8, stride=2 * PLANES), :]
                )
        for k in range(4):
            target[1904 + 240 * k : 2144 + 240 * k] = speed_ref[skip + k]
            for half in range(2):
                start = 2864 + 16 * k + 8 * half
                target[start : start + 8] = (
                    slab_ref[other + k, half] + slab_other_ref[other + k, half]
                )


def faces(*arrays):
    vmem = pl.BlockSpec(memory_space=pltpu.VMEM)
    return pl.pallas_call(
        faces_kernel,
        out_shape=(jax.ShapeDtypeStruct((2928, 128), jnp.float32),) * 2,
        in_specs=[vmem] * 8,
        out_specs=(vmem, vmem),
        compiler_params=pltpu.CompilerParams(vmem_limit_bytes=24 * 1024 * 1024),
        name="faces",
    )(*arrays)


def cut_kernel(main_ref, up_ref, down_ref, done):
    copies = []
    for c in range(3):
        for k, (target, start) in enumerate(((up_ref, 1920), (down_ref, 0))):
            copies.append(
                pltpu.make_async_copy(
                    main_ref.at[pl.ds(2048 * c + start, 128)],
                    target.at[pl.ds(128 * c, 128)],
                    done.at[2 * c + k],
                )
            )
    for copy in copies:
        copy.start()
    for copy in copies:
        copy.wait()


def cut_velocity(main):
    vmem = pl.BlockSpec(memory_space=pltpu.VMEM)
    return pl.pallas_call(
        cut_kernel,
        out_shape=(jax.ShapeDtypeStruct((384, 128), jnp.float32),) * 2,
        in_specs=[pl.BlockSpec(memory_space=pl.ANY)],
        out_specs=(vmem, vmem),
        scratch_shapes=[pltpu.SemaphoreType.DMA((6,))],
        name="cut_velocity",
    )(main)


def velocity_rows(main_ref, low_ref, high_ref, y, c):
    blank = jnp.zeros((4, 128), jnp.float32)
    return jnp.concatenate(
        [
            blank,
            low_ref[pl.ds(128 * c + y, 4, stride=32), :],
            main_ref[pl.ds(2048 * c + y, 64, stride=32), :],
            high_ref[pl.ds(128 * c + y, 4, stride=32), :],
            blank,
        ],
        0,
    )


def velocity_kernel(
    side_ref, main_ref, low_ref, high_ref, slab_ref, first_ref, last_ref, gather_ref
):
    upper = side_ref[0] == 0
    lane = lax.broadcasted_iota(jnp.int32, (GROUP, 128), 1)
    target = jnp.where(upper, 0, 4)
    gather_ref[ROWS:256] = jnp.zeros((256 - ROWS, 128), jnp.float32)

    def sixteen(turn, carry):
        for c in range(3):
            gathered = jnp.zeros((GROUP, 128), jnp.float32)
            for k in range(16):
                rows = velocity_rows(main_ref, low_ref, high_ref, 16 * turn + k, c)
                moved = pltpu.roll(rows, (8 * k + 4) % 128, 1)
                goal = 8 * k + target
                gathered = jnp.where((lane >= goal) & (lane < goal + 4), moved, gathered)
            gather_ref[GROUP * c : GROUP * c + GROUP] = gathered
        slabs = jnp.transpose(gather_ref[...])
        for half in range(2):
            slab_ref[pl.ds(16 * turn, 16), half] = slabs[
                :, 128 * half : 128 * half + 128
            ].reshape(16, 8, 128)
        return carry

    lax.fori_loop(0, 2, sixteen, 0)
    for k in range(7):
        for c in range(3):
            rows = slice(GROUP * c, GROUP * c + GROUP)
            first_ref[k, rows] = velocity_rows(main_ref, low_ref, high_ref, k, c)
            last_ref[k, rows] = velocity_rows(main_ref, low_ref, high_ref, 25 + k, c)


def arrange_velocity(side, main, low, high):
    vmem = pl.BlockSpec(memory_space=pltpu.VMEM)
    smem = pl.BlockSpec(memory_space=pltpu.SMEM)
    return pl.pallas_call(
        velocity_kernel,
        out_shape=(
            jax.ShapeDtypeStruct((32, 2, 8, 128), jnp.float32),
            jax.ShapeDtypeStruct((7, ROWS, 128), jnp.float32),
            jax.ShapeDtypeStruct((7, ROWS, 128), jnp.float32),
        ),
        in_specs=[smem, vmem, vmem, vmem],
        out_specs=(vmem, vmem, vmem),
        scratch_shapes=[pltpu.VMEM((256, 128), jnp.float32)],
        compiler_params=pltpu.CompilerParams(vmem_limit_bytes=16 * 1024 * 1024),
        cost_estimate=pl.CostEstimate(
            flops=4_000_000_000, bytes_accessed=8_000_000, transcendentals=0
        ),
        name="arrange_velocity",
    )(side, main, low, high)


def bands(upper, odd):
    source = lax.broadcasted_iota(jnp.int32, (128, 128), 0)
    target = lax.broadcasted_iota(jnp.int32, (128, 128), 1)

    def entries(distance):
        near = jnp.where(distance == 1, 8.0 if odd else 16.0, 0.0)
        near = jnp.where(distance == -1, -8.0 if odd else 16.0, near)
        near = jnp.where(distance == 2, -1.0, near)
        return jnp.where(distance == -2, 1.0 if odd else -1.0, near)

    main = entries(source - target).astype(jnp.bfloat16)
    layer = source % 8
    begin = jnp.where(upper, 4, 0)
    outer = (layer >= begin) & (layer < begin + 4)
    halo = jnp.where(outer, entries(layer + jnp.where(upper, 124, -4) - target), 0.0)
    return main, halo, source // 8


SCALE_L = 0.1 * 0.5 / 12.0
SCALE_D = 0.1 / 12.0


def fill_bands(upper, even_ref, odd_ref):
    for odd, ref in ((False, even_ref), (True, odd_ref)):
        main, halo, owner = bands(upper, odd)
        for k in range(16):
            ref[k, 0:128] = main
            ref[k, 128:256] = jnp.where(owner == k, halo, 0.0).astype(jnp.bfloat16)


def row_mask(place_ref):
    row = lax.broadcasted_iota(jnp.int32, (GROUP, 128), 0)
    start = jnp.where(place_ref[0] == 0, 8, 0)
    stop = jnp.where(place_ref[0] == place_ref[1] - 1, 72, GROUP)
    return jnp.where((row >= start) & (row < stop), 1.0, 0.0)


def lane_mask(place_ref):
    lane = lax.broadcasted_iota(jnp.int32, (8, 256), 1)
    column = lane % GROUP
    start = jnp.where(place_ref[0] == 0, 8, 0)
    stop = jnp.where(place_ref[0] == place_ref[1] - 1, 72, GROUP)
    mask = jnp.where((column >= start) & (column < stop), 1.0, 0.0)
    return jnp.where(lane < ROWS, mask, 0.0)


def own_slab(near_ref, swapped_ref, plane):
    return jnp.concatenate(
        [
            near_ref[pl.ds(half * PLANES + plane, 8, stride=2 * PLANES), :]
            + swapped_ref[pl.ds(half * PLANES + plane, 8, stride=2 * PLANES), :]
            for half in range(2)
        ],
        1,
    )


def place_mesh(w_ref, a_ref, index, plane, main, slab, upper, inside, inside_slab):
    layer = lax.broadcasted_iota(jnp.int32, (8, 256), 0)
    slab = slab * inside_slab
    a_ref[plane] = slab
    inner = pltpu.roll(slab, 4, 0)
    bottom = jnp.where((layer < 4) & (layer < jnp.where(upper, 0, 8)), inner, main[0:8])
    top = jnp.where((layer >= 4) & (layer < jnp.where(upper, 8, 0)), inner, main[120:128])
    turned = jnp.transpose(jnp.concatenate([bottom, main[8:120], top], 0))
    zeros = jnp.zeros((8, 128), jnp.float32)
    w_ref[index, 0:8] = zeros
    w_ref[index, 248:256] = zeros
    for c in range(3):
        rows = slice(GROUP * c, GROUP * c + GROUP)
        w_ref[index, 8 + GROUP * c : 88 + GROUP * c] = turned[rows] * inside


def place_speed(v_ref, index, main):
    zeros = jnp.zeros((8, 128), jnp.float32)
    v_ref[index, 0:8] = zeros
    v_ref[index, 248:256] = zeros
    v_ref[index, 8:248] = main


def turn_slabs(source_ref, target_ref, groups):
    for g in range(groups):
        stacked = jnp.concatenate([source_ref[16 * g + k] for k in range(16)], 0)
        target_ref[g] = jnp.transpose(stacked)[:ROWS].astype(jnp.bfloat16)


def along_z(main, halo, matrix):
    return jnp.dot(
        jnp.concatenate([main.astype(jnp.bfloat16), halo], 1), matrix,
        preferred_element_type=jnp.float32,
    )


def part(ref, index, c, dx):
    start = 8 + GROUP * c + dx
    return ref[index, start : start + GROUP]


def curvature(ref, at, c):
    near = part(ref, at(1), c, 0) + part(ref, at(-1), c, 0) + (
        part(ref, at(0), c, 1) + part(ref, at(0), c, -1)
    )
    far = part(ref, at(2), c, 0) + part(ref, at(-2), c, 0) + (
        part(ref, at(0), c, 2) + part(ref, at(0), c, -2)
    )
    return 16.0 * near - far


def first_plane(w_ref, w_at, v_ref, v_at, curve, climb, c, centre):
    rows = slice(GROUP * c, GROUP * c + GROUP)
    here = v_at(0)
    slope_x = 8.0 * (part(v_ref, here, c, 1) - part(v_ref, here, c, -1)) - (
        part(v_ref, here, c, 2) - part(v_ref, here, c, -2)
    )
    slope_y = 8.0 * (part(v_ref, v_at(1), c, 0) - part(v_ref, v_at(-1), c, 0)) - (
        part(v_ref, v_at(2), c, 0) - part(v_ref, v_at(-2), c, 0)
    )
    slopes = (slope_x, slope_y, climb[rows])
    stretch = centre[0] * slopes[0] + centre[1] * slopes[1] + centre[2] * slopes[2]
    result = (
        centre[c] * (1.0 - 90.0 * SCALE_L)
        + SCALE_L * (curvature(w_ref, w_at, c) + curve[rows])
        + SCALE_D * stretch
    )
    return result, slopes


def interior_kernel(
    place_ref, *refs
):
    sources, (f_out_ref, d_out_ref, w_edge_ref), held = refs[:8], refs[8:11], refs[11:19]
    w_ref, wt_ref, a_ref, v_ref, vt_ref, b_ref, even_ref, odd_ref, f_ref, d_ref, done = refs[19:]
    grid_ref, near_ref, swapped_ref, slab_ref, slab_other_ref, main_ref, behind_ref, ahead_ref = held
    fetches = [
        pltpu.make_async_copy(sources[k], held[k], done.at[2 + k]) for k in range(8)
    ]
    for fetch in fetches:
        fetch.start()
    upper = place_ref[4] == 0
    inside = row_mask(place_ref)
    inside_slab = lane_mask(place_ref)
    fill_bands(upper, even_ref, odd_ref)

    def mesh_plane(plane, carry):
        main = jnp.concatenate(
            [
                grid_ref[pl.ds(half * PLANES + plane, 128, stride=2 * PLANES), :]
                for half in range(2)
            ],
            1,
        )
        slab = own_slab(near_ref, swapped_ref, plane)
        place_mesh(w_ref, a_ref, plane - 7, plane, main, slab, upper, inside, inside_slab)
        return carry

    blank = jnp.zeros((8, 256), jnp.float32)
    for plane in tuple(range(7)) + tuple(range(33, 48)):
        a_ref[plane] = blank
    for plane in tuple(range(4)) + tuple(range(36, 48)):
        b_ref[plane] = blank
    for fetch in fetches[:3]:
        fetch.wait()
    lax.fori_loop(7, 33, mesh_plane, 0, unroll=2)

    def speed_plane(plane, carry):
        place_speed(
            v_ref, plane,
            jnp.concatenate(
                [velocity_rows(main_ref, behind_ref, ahead_ref, plane, c) for c in range(3)], 0
            ),
        )
        slab = slab_ref[plane] + slab_other_ref[plane]
        b_ref[plane + 4] = jnp.concatenate([slab[0], slab[1]], 1)
        return carry

    for fetch in fetches[3:]:
        fetch.wait()
    lax.fori_loop(0, 32, speed_plane, 0)
    turn_slabs(a_ref, wt_ref, 2)
    turn_slabs(b_ref, vt_ref, 2)
    for k in range(4):
        w_edge_ref[k] = w_ref[k]
        w_edge_ref[4 + k] = w_ref[22 + k]

    def step(k, carry):
        y = k + 9
        curve = along_z(w_ref[y - 7, 8:248], wt_ref[y >> 4], even_ref[y & 15])
        climb = along_z(v_ref[y - 4, 8:248], vt_ref[y >> 4], odd_ref[y & 15])
        zeros = jnp.zeros((8, 128), jnp.float32)
        f_ref[k, 0:8] = zeros
        f_ref[k, 248:256] = zeros
        centre = [part(w_ref, y - 7, c, 0) for c in range(3)]
        for c in range(3):
            result, slopes = first_plane(
                w_ref, lambda o: y - 7 + o, v_ref, lambda o: y - 4 + o, curve, climb, c, centre
            )
            for d in range(3):
                d_ref[k, d, GROUP * c : GROUP * c + GROUP] = slopes[d].astype(jnp.bfloat16)
            f_ref[k, 8 + GROUP * c : 88 + GROUP * c] = result * inside
        return carry

    lax.fori_loop(0, 22, step, 0, unroll=2)
    copies = [
        pltpu.make_async_copy(f_ref, f_out_ref, done.at[0]),
        pltpu.make_async_copy(d_ref, d_out_ref, done.at[1]),
    ]
    for copy in copies:
        copy.start()
    for copy in copies:
        copy.wait()


def interior(*arrays):
    vmem = pl.BlockSpec(memory_space=pltpu.VMEM)
    smem = pl.BlockSpec(memory_space=pltpu.SMEM)
    scratch = [
        pltpu.VMEM((256 * PLANES, 128), jnp.float32),
        pltpu.VMEM((16 * PLANES, 128), jnp.float32),
        pltpu.VMEM((16 * PLANES, 128), jnp.float32),
        pltpu.VMEM((32, 2, 8, 128), jnp.float32),
        pltpu.VMEM((32, 2, 8, 128), jnp.float32),
        pltpu.VMEM((6144, 128), jnp.float32),
        pltpu.VMEM((384, 128), jnp.float32),
        pltpu.VMEM((384, 128), jnp.float32),
        pltpu.VMEM((26, 256, 128), jnp.float32),
        pltpu.VMEM((2, ROWS, 128), jnp.bfloat16),
        pltpu.VMEM((48, 8, 256), jnp.float32),
        pltpu.VMEM((32, 256, 128), jnp.float32),
        pltpu.VMEM((2, ROWS, 128), jnp.bfloat16),
        pltpu.VMEM((48, 8, 256), jnp.float32),
        pltpu.VMEM((16, 256, 128), jnp.bfloat16),
        pltpu.VMEM((16, 256, 128), jnp.bfloat16),
        pltpu.VMEM((22, 256, 128), jnp.float32),
        pltpu.VMEM((22, 3, ROWS, 128), jnp.bfloat16),
        pltpu.SemaphoreType.DMA((10,)),
    ]
    anywhere = pl.BlockSpec(memory_space=pl.ANY)
    return pl.pallas_call(
        interior_kernel,
        out_shape=(
            jax.ShapeDtypeStruct((22, 256, 128), jnp.float32),
            jax.ShapeDtypeStruct((22, 3, ROWS, 128), jnp.bfloat16),
            jax.ShapeDtypeStruct((8, 256, 128), jnp.float32),
        ),
        in_specs=[smem] + [anywhere] * 8,
        out_specs=(anywhere, anywhere, vmem),
        scratch_shapes=scratch,
        compiler_params=pltpu.CompilerParams(vmem_limit_bytes=34 * 1024 * 1024),
        cost_estimate=pl.CostEstimate(
            flops=15_000_000_000, bytes_accessed=40_000_000, transcendentals=0
        ),
        name="interior",
    )(*arrays)


def edges_kernel(
    place_ref, f_in_ref, d_in_ref, w_edge_ref, speed_low_ref, speed_high_ref,
    near_ref, swapped_ref, slab_ref, slab_other_ref, own_high_ref, own_low_ref, low_ref, high_ref,
    out_ref, w_ref, wt_ref, a_ref, v_ref, vt_ref, b_ref, f_ref, e_ref, even_ref, odd_ref, d_ref, d_mid_ref, done,
):
    copies = [
        pltpu.make_async_copy(f_in_ref, f_ref.at[pl.ds(7, 22)], done.at[0]),
        pltpu.make_async_copy(d_in_ref, d_mid_ref, done.at[1]),
    ]
    for copy in copies:
        copy.start()
    upper = place_ref[4] == 0
    inside = row_mask(place_ref)
    inside_slab = lane_mask(place_ref)
    keep_low = jnp.where(place_ref[2] == 0, 0.0, 1.0)
    keep_high = jnp.where(place_ref[2] == place_ref[3] - 1, 0.0, 1.0)
    fill_bands(upper, even_ref, odd_ref)

    def block(ref, k, start, stop):
        base = 272 * k
        return jnp.concatenate(
            [ref[base + start : base + stop], ref[base + 136 + start : base + 136 + stop]], 1
        )

    for plane in range(7):
        for ref, own_ref, k, own_k, at, keep in (
            (low_ref, own_low_ref, plane, plane - 1, plane, keep_low if plane < 4 else None),
            (high_ref, own_high_ref, plane, plane + 1, plane + 33, keep_high if plane >= 3 else None),
        ):
            main, slab = block(ref, k, 0, 128), block(ref, k, 128, 136)
            if 0 <= own_k < 7:
                main, slab = main + block(own_ref, own_k, 0, 128), slab + block(own_ref, own_k, 128, 136)
            else:
                slab = slab + own_slab(near_ref, swapped_ref, at)
            if keep is not None:
                main, slab = main * keep, slab * keep
            index = at if at < 20 else at - 18
            place_mesh(w_ref, a_ref, index, at, main, slab, upper, inside, inside_slab)
    for k in range(4):
        w_ref[7 + k] = w_edge_ref[k]
        w_ref[11 + k] = w_edge_ref[4 + k]

    def middle_slab(plane, carry):
        a_ref[plane] = own_slab(near_ref, swapped_ref, plane) * inside_slab
        return carry

    lax.fori_loop(7, 33, middle_slab, 0, unroll=2)
    for ref, begin, index in ((low_ref, 0, 0), (high_ref, 36, 18)):
        for k in range(4):
            start, end = 1904 + 240 * k, 2864 + 16 * k
            place_speed(v_ref, index + k, ref[start : start + 240])
            b_ref[begin + k] = jnp.concatenate([ref[end : end + 8], ref[end + 8 : end + 16]], 1)
    for k in range(7):
        place_speed(v_ref, 4 + k, speed_low_ref[k])
        place_speed(v_ref, 11 + k, speed_high_ref[k])

    def speed_slab(plane, carry):
        slab = slab_ref[plane] + slab_other_ref[plane]
        b_ref[plane + 4] = jnp.concatenate([slab[0], slab[1]], 1)
        return carry

    lax.fori_loop(0, 32, speed_slab, 0, unroll=4)
    blank = jnp.zeros((8, 256), jnp.float32)
    for k in range(40, 48):
        a_ref[k] = blank
        b_ref[k] = blank
    turn_slabs(a_ref, wt_ref, 3)
    turn_slabs(b_ref, vt_ref, 3)

    for copy in copies:
        copy.wait()

    def first_steps(start, lag, lag_f, lag_d, keep, outside, stored):
        def step(k, carry):
            y = k + start
            curve = along_z(w_ref[y - lag, 8:248], wt_ref[y >> 4], even_ref[y & 15])
            climb = along_z(v_ref[y - lag, 8:248], vt_ref[y >> 4], odd_ref[y & 15])
            zeros = jnp.zeros((8, 128), jnp.float32)
            scale = jnp.where((k >= outside[0]) & (k < outside[1]), keep, 1.0)
            f_ref[y - lag_f, 0:8] = zeros
            f_ref[y - lag_f, 248:256] = zeros
            centre = [part(w_ref, y - lag, c, 0) for c in range(3)]
            at = lambda o: y - lag + o
            for c in range(3):
                result, slopes = first_plane(w_ref, at, v_ref, at, curve, climb, c, centre)
                for d in range(3):
                    d_ref[y - lag_d, d, GROUP * c : GROUP * c + GROUP] = slopes[d].astype(jnp.bfloat16)
                f_ref[y - lag_f, 8 + GROUP * c : 88 + GROUP * c] = result * (inside * scale)
            return carry

        lax.fori_loop(0, 7, step, 0, unroll=stored)

    first_steps(2, 0, 2, 2, keep_low, (0, 2), 1)
    first_steps(31, 18, 2, 24, keep_high, (5, 7), 1)

    lane = lax.broadcasted_iota(jnp.int32, (8, 256), 1)
    group = lane // GROUP

    def slab_step(k, carry):
        y = k + 4
        here = a_ref[y]
        speed = b_ref[y]

        def both_ways(array, step, axis):
            size = array.shape[axis]
            return pltpu.roll(array, size - step, axis), pltpu.roll(array, step, axis)

        ax1, bx1 = both_ways(here, 1, 1)
        ax2, bx2 = both_ways(here, 2, 1)
        az1, bz1 = both_ways(here, 1, 0)
        az2, bz2 = both_ways(here, 2, 0)
        near = a_ref[y + 1] + a_ref[y - 1] + (ax1 + bx1) + (az1 + bz1)
        far = a_ref[y + 2] + a_ref[y - 2] + (ax2 + bx2) + (az2 + bz2)
        vx1, ux1 = both_ways(speed, 1, 1)
        vx2, ux2 = both_ways(speed, 2, 1)
        vz1, uz1 = both_ways(speed, 1, 0)
        vz2, uz2 = both_ways(speed, 2, 0)
        slope_x = 8.0 * (vx1 - ux1) - (vx2 - ux2)
        slope_y = 8.0 * (b_ref[y + 1] - b_ref[y - 1]) - (b_ref[y + 2] - b_ref[y - 2])
        slope_z = 8.0 * (vz1 - uz1) - (vz2 - uz2)
        right1 = pltpu.roll(here, GROUP, 1)
        right2 = pltpu.roll(here, 2 * GROUP, 1)
        left1 = pltpu.roll(here, 256 - GROUP, 1)
        left2 = pltpu.roll(here, 256 - 2 * GROUP, 1)
        swirl_x = jnp.where(group == 0, here, jnp.where(group == 1, right1, right2))
        swirl_y = jnp.where(group == 0, left1, jnp.where(group == 1, here, right1))
        swirl_z = jnp.where(group == 0, left2, jnp.where(group == 1, left1, here))
        e_ref[k] = (
            here * (1.0 - 90.0 * SCALE_L)
            + SCALE_L * (16.0 * near - far)
            + SCALE_D * (swirl_x * slope_x + swirl_y * slope_y + swirl_z * slope_z)
        )
        return carry

    lax.fori_loop(0, 32, slab_step, 0, unroll=2)
    turn_slabs(e_ref, vt_ref, 2)

    def second(slopes_ref, index, k):
        y = k + 2
        curve = along_z(f_ref[y, 8:248], vt_ref[k >> 4], even_ref[k & 15])
        centre = [part(f_ref, y, c, 0) for c in range(3)]
        for c in range(3):
            rows = slice(GROUP * c, GROUP * c + GROUP)
            slopes = [slopes_ref[index, d, rows].astype(jnp.float32) for d in range(3)]
            stretch = centre[0] * slopes[0] + centre[1] * slopes[1] + centre[2] * slopes[2]
            result = (
                centre[c] * (1.0 - 90.0 * SCALE_L)
                + SCALE_L * (curvature(f_ref, lambda o: y + o, c) + curve[rows])
                + SCALE_D * stretch
            )
            out_ref[pl.ds(2048 * c + k, 64, stride=32), :] = result[8:72]

    def second_low(k, carry):
        second(d_ref, k + 2, k)
        return carry

    def second_high(k, carry):
        second(d_ref, k - 20, k)
        return carry

    def second_middle(k, carry):
        second(d_mid_ref, k - 5, k)
        return carry

    lax.fori_loop(0, 5, second_low, 0)
    lax.fori_loop(27, 32, second_high, 0)
    lax.fori_loop(5, 27, second_middle, 0, unroll=2)


def edges(*arrays):
    vmem = pl.BlockSpec(memory_space=pltpu.VMEM)
    smem = pl.BlockSpec(memory_space=pltpu.SMEM)
    scratch = [
        pltpu.VMEM((22, 256, 128), jnp.float32),
        pltpu.VMEM((3, ROWS, 128), jnp.bfloat16),
        pltpu.VMEM((48, 8, 256), jnp.float32),
        pltpu.VMEM((22, 256, 128), jnp.float32),
        pltpu.VMEM((3, ROWS, 128), jnp.bfloat16),
        pltpu.VMEM((48, 8, 256), jnp.float32),
        pltpu.VMEM((36, 256, 128), jnp.float32),
        pltpu.VMEM((32, 8, 256), jnp.float32),
        pltpu.VMEM((16, 256, 128), jnp.bfloat16),
        pltpu.VMEM((16, 256, 128), jnp.bfloat16),
        pltpu.VMEM((14, 3, ROWS, 128), jnp.bfloat16),
        pltpu.VMEM((22, 3, ROWS, 128), jnp.bfloat16),
        pltpu.SemaphoreType.DMA((2,)),
    ]
    anywhere = pl.BlockSpec(memory_space=pl.ANY)
    return pl.pallas_call(
        edges_kernel,
        out_shape=jax.ShapeDtypeStruct((3 * 64 * 32, 128), jnp.float32),
        in_specs=[smem, anywhere, anywhere] + [vmem] * 11,
        out_specs=vmem,
        scratch_shapes=scratch,
        compiler_params=pltpu.CompilerParams(vmem_limit_bytes=38 * 1024 * 1024),
        name="edges",
    )(*arrays)


def sort_inputs(strength, fraction, stream_cell, span_cell, height_cell):
    key = ((height_cell + 2) << 16) | ((stream_cell + 2) << 8) | (span_cell + 2)
    load = strength.astype(jnp.float32)
    return lax.sort(
        (key, load[0], load[1], load[2], fraction[0], fraction[1], fraction[2]),
        num_keys=1, is_stable=False,
    )


def pack_kernel(key_ref, *refs):
    fields, packed_ref = refs[:6], refs[6]
    key = key_ref[...]
    cells = ((key >> 8) & 255, key & 255, key >> 16)
    for f in range(6):
        packed_ref[64 * f : 64 * f + 64] = fields[f][...]
    for f in range(3):
        packed_ref[384 + 64 * f : 448 + 64 * f] = (cells[f] - 2).astype(jnp.float32)


def pack(parts):
    vmem = pl.BlockSpec(memory_space=pltpu.VMEM)
    return pl.pallas_call(
        pack_kernel,
        out_shape=jax.ShapeDtypeStruct((576, 128), jnp.float32),
        in_specs=[vmem] * 7,
        out_specs=vmem,
        compiler_params=pltpu.CompilerParams(vmem_limit_bytes=16 * 1024 * 1024),
        name="pack",
    )(*[p.reshape(64, 128) for p in parts])


def shards(strength, fraction, stream_cell, span_cell, height_cell, velocity):
    count_x, count_y = lax.axis_size("gx"), lax.axis_size("gy")
    index_x, index_y, index_z = (lax.axis_index(a) for a in ("gx", "gy", "gz"))
    side = index_z.astype(jnp.int32).reshape(1)
    place = jnp.stack(
        [index_x, jnp.int32(count_x), index_y, jnp.int32(count_y), index_z]
    ).astype(jnp.int32)
    up_x = [(i, i + 1) for i in range(count_x - 1)]
    down_x = [(j, i) for i, j in up_x]
    up_y = [(i, i + 1) for i in range(count_y - 1)]
    velocity = velocity.reshape(6144, 128)
    upward, downward = cut_velocity(velocity)
    low_speed = lax.ppermute(upward, "gx", up_x)
    high_speed = lax.ppermute(downward, "gx", down_x)
    parts = sort_inputs(strength, fraction, stream_cell, span_cell, height_cell)
    packed = pack(parts)
    low = lax.ppermute(packed, "gx", up_x)
    high = lax.ppermute(packed, "gx", down_x)

    def limits(block):
        span = block[512:576].reshape(32, 256)
        return jnp.stack([span[:, 0], span[:, 255]]).astype(jnp.int32)

    speed_slab, speed_first, speed_last = arrange_velocity(side, velocity, low_speed, high_speed)
    swap = [(0, 1), (1, 0)]
    other_slab = lax.ppermute(speed_slab, "gz", swap)
    bounds = jnp.stack([limits(packed), limits(low), limits(high)])
    grid, near, up_mesh, down_mesh = deposit(bounds, side, packed, low, high)
    swapped = lax.ppermute(near, "gz", swap)
    to_high, to_low = faces(
        up_mesh, down_mesh, near, swapped, speed_first, speed_last, speed_slab, other_slab
    )
    from_low = lax.ppermute(to_high, "gy", up_y)
    from_high = lax.ppermute(to_low, "gy", [(j, i) for i, j in up_y])
    grid = grid.reshape(256 * PLANES, 128)
    middle, slopes, mesh_edges = interior(
        place, grid, near, swapped, speed_slab, other_slab, velocity, low_speed, high_speed
    )
    out = edges(
        place, middle, slopes, mesh_edges, speed_first, speed_last, near, swapped,
        speed_slab, other_slab, to_high, to_low, from_low, from_high,
    )
    return out.reshape(3, 64, 32, 128)


def solution(mesh):
    return jax.shard_map(
        shards,
        mesh=mesh,
        in_specs=(
            P(None, ("gx", "gy", "gz")),
            P(None, ("gx", "gy", "gz")),
            P(("gx", "gy", "gz")),
            P(("gx", "gy", "gz")),
            P(("gx", "gy", "gz")),
            P(None, "gx", "gy", "gz"),
        ),
        out_specs=P(None, "gx", "gy", "gz"),
        check_vma=False,
    )
```

```python
import functools

import jax
import jax.numpy as jnp
from jax import lax
from jax.experimental import pallas as pl
from jax.experimental.pallas import tpu as pltpu
from jax.sharding import PartitionSpec as P

GROUP = 80
ROWS = 240
PLANES = 40
DEPTH = 144
WINDOW = 10
LAYERS = DEPTH + 5


def kernel_weights(fraction):
    remainder = 1.0 - fraction
    return (
        -0.5 * fraction * remainder * remainder,
        1.0 - 2.5 * fraction * fraction + 1.5 * fraction * fraction * fraction,
        1.0 - 2.5 * remainder * remainder + 1.5 * remainder * remainder * remainder,
        -0.5 * fraction * fraction * remainder,
    )


def choose(distance, weights):
    total = jnp.where(distance == 3, weights[3], 0.0)
    for offset in (2, 1, 0):
        total = jnp.where(distance == offset, weights[offset], total)
    return total


def add_source(bounds_ref, number, ref, shift, grid_ref):
    start_x, count_x = {0: (0, GROUP), -64: (0, 16), 64: (64, 16)}[shift]
    rows_x = lax.broadcasted_iota(jnp.int32, (count_x, 128), 0) + start_x
    below = jnp.zeros((start_x, 128), jnp.bfloat16)
    above = jnp.zeros((GROUP - start_x - count_x, 128), jnp.bfloat16)
    rows_y = lax.broadcasted_iota(jnp.int32, (PLANES, 128), 0)
    owner = lax.broadcasted_iota(jnp.int32, (8, 128), 0) // 2

    def group(turn, carry):
        field = [ref[pl.ds(64 * f + 8 * turn, 8), :] for f in range(9)]
        weight_x = kernel_weights(field[3])
        weight_y = kernel_weights(field[4])
        weight_z = kernel_weights(field[5])
        cell_x = field[6].astype(jnp.int32) + (7 + shift)
        cell_y = field[7].astype(jnp.int32) + 3
        cell_z = field[8].astype(jnp.int32) + 7
        low = [bounds_ref[number, 0, 4 * turn + k] + 7 for k in range(4)]
        high = [bounds_ref[number, 1, 4 * turn + k] + 10 for k in range(4)]
        turns = functools.reduce(
            jnp.maximum, [(high[k] - low[k] + WINDOW) // WINDOW for k in range(4)]
        )

        def window(step, inner):
            bases = [jnp.minimum(low[k] + step * WINDOW, DEPTH - 5) for k in range(4)]
            origin = jnp.full((8, 128), bases[0], jnp.int32)
            for k in range(1, 4):
                origin = jnp.where(owner == k, bases[k], origin)
            origin = origin - cell_z
            tall = [choose(origin + j, weight_z) for j in range(WINDOW)]
            for k in range(4):
                leads, crosses = [], []
                for half in (2 * k, 2 * k + 1):
                    row = slice(half, half + 1)
                    spread_x = choose(rows_x - cell_x[row], [w[row] for w in weight_x])
                    spread_y = choose(rows_y - cell_y[row], [w[row] for w in weight_y])
                    leads.append(
                        jnp.concatenate(
                            [
                                part
                                for c in range(3)
                                for part in (
                                    below, (field[c][row] * spread_x).astype(jnp.bfloat16), above
                                )
                                if part.shape[0]
                            ]
                            + [jnp.zeros((16, 128), jnp.bfloat16)],
                            0,
                        )
                    )
                    crosses.append(
                        jnp.concatenate(
                            [
                                jnp.concatenate(
                                    [tall[j][row] * spread_y, tall[j + 1][row] * spread_y], 0
                                ).astype(jnp.bfloat16)
                                for j in range(0, WINDOW, 2)
                            ],
                            0,
                        )
                    )
                product = lax.dot_general(
                    jnp.concatenate(crosses, 1), jnp.concatenate(leads, 1),
                    (((1,), (1,)), ((), ())), preferred_element_type=jnp.float32,
                )
                for j in range(WINDOW):
                    for half in range(2):
                        grid_ref[bases[k] + j, half] += product[
                            PLANES * j : PLANES * j + PLANES, 128 * half : 128 * half + 128
                        ]
            return inner

        lax.fori_loop(0, turns, window, 0)
        return carry

    lax.fori_loop(0, 8, group, 0)


def deposit_kernel(
    bounds_ref, side_ref, own_ref, low_ref, high_ref, grid_ref, near_ref, up_ref, down_ref
):
    def clear(layer, carry):
        grid_ref[layer] = jnp.zeros((2, PLANES, 128), jnp.float32)
        return carry

    lax.fori_loop(0, LAYERS, clear, 0)
    add_source(bounds_ref, 0, own_ref, 0, grid_ref)
    add_source(bounds_ref, 1, low_ref, -64, grid_ref)
    add_source(bounds_ref, 2, high_ref, 64, grid_ref)
    flat_ref = grid_ref.reshape(2 * LAYERS * PLANES, 128)
    inner = jnp.where(side_ref[0] == 0, 132, 4)
    for layer in range(8):
        for half in range(2):
            start = PLANES * (2 * layer + half)
            near_ref[start : start + PLANES] = grid_ref[inner + layer, half]
    for target, plane in ((up_ref, 32), (down_ref, 1)):
        for k in range(7):
            for half in range(2):
                start = 256 * k + 128 * half
                target[start : start + 128] = flat_ref[
                    pl.ds((16 + half) * PLANES + plane + k, 128, stride=2 * PLANES), :
                ]


def deposit(bounds, side, own, low, high):
    vmem = pl.BlockSpec(memory_space=pltpu.VMEM)
    smem = pl.BlockSpec(memory_space=pltpu.SMEM)
    return pl.pallas_call(
        deposit_kernel,
        out_shape=(
            jax.ShapeDtypeStruct((LAYERS, 2, PLANES, 128), jnp.float32),
            jax.ShapeDtypeStruct((16 * PLANES, 128), jnp.float32),
            jax.ShapeDtypeStruct((1792, 128), jnp.float32),
            jax.ShapeDtypeStruct((1792, 128), jnp.float32),
        ),
        in_specs=[smem, smem, vmem, vmem, vmem],
        out_specs=(vmem,) * 4,
        compiler_params=pltpu.CompilerParams(vmem_limit_bytes=24 * 1024 * 1024),
        cost_estimate=pl.CostEstimate(
            flops=16_000_000_000, bytes_accessed=40_000_000, transcendentals=0
        ),
        name="deposit",
    )(bounds, side, own, low, high)


def faces_kernel(
    up_own_ref, down_own_ref, near_ref, swapped_ref, first_ref, last_ref, slab_ref, slab_other_ref,
    up_ref, down_ref,
):
    for target, own, plane, other, speed_ref, skip in (
        (up_ref, up_own_ref, 32, 28, last_ref, 3), (down_ref, down_own_ref, 1, 0, first_ref, 0)
    ):
        for k in range(7):
            for half in range(2):
                start = 272 * k + 136 * half
                first = PLANES * half + plane + k
                block = 256 * k + 128 * half
                target[start : start + 128] = own[block : block + 128]
                target[start + 128 : start + 136] = (
                    near_ref[pl.ds(first, 8, stride=2 * PLANES), :]
                    + swapped_ref[pl.ds(first, 8, stride=2 * PLANES), :]
                )
        for k in range(4):
            target[1904 + 240 * k : 2144 + 240 * k] = speed_ref[skip + k]
            for half in range(2):
                start = 2864 + 16 * k + 8 * half
                target[start : start + 8] = (
                    slab_ref[other + k, half] + slab_other_ref[other + k, half]
                )


def faces(*arrays):
    vmem = pl.BlockSpec(memory_space=pltpu.VMEM)
    return pl.pallas_call(
        faces_kernel,
        out_shape=(jax.ShapeDtypeStruct((2928, 128), jnp.float32),) * 2,
        in_specs=[vmem] * 8,
        out_specs=(vmem, vmem),
        compiler_params=pltpu.CompilerParams(vmem_limit_bytes=24 * 1024 * 1024),
        name="faces",
    )(*arrays)


def cut_kernel(main_ref, up_ref, down_ref, done):
    copies = []
    for c in range(3):
        for k, (target, start) in enumerate(((up_ref, 1920), (down_ref, 0))):
            copies.append(
                pltpu.make_async_copy(
                    main_ref.at[pl.ds(2048 * c + start, 128)],
                    target.at[pl.ds(128 * c, 128)],
                    done.at[2 * c + k],
                )
            )
    for copy in copies:
        copy.start()
    for copy in copies:
        copy.wait()


def cut_velocity(main):
    vmem = pl.BlockSpec(memory_space=pltpu.VMEM)
    return pl.pallas_call(
        cut_kernel,
        out_shape=(jax.ShapeDtypeStruct((384, 128), jnp.float32),) * 2,
        in_specs=[pl.BlockSpec(memory_space=pl.ANY)],
        out_specs=(vmem, vmem),
        scratch_shapes=[pltpu.SemaphoreType.DMA((6,))],
        name="cut_velocity",
    )(main)


def velocity_rows(main_ref, low_ref, high_ref, y, c):
    blank = jnp.zeros((4, 128), jnp.float32)
    return jnp.concatenate(
        [
            blank,
            low_ref[pl.ds(128 * c + y, 4, stride=32), :],
            main_ref[pl.ds(2048 * c + y, 64, stride=32), :],
            high_ref[pl.ds(128 * c + y, 4, stride=32), :],
            blank,
        ],
        0,
    )


def velocity_kernel(
    side_ref, main_ref, low_ref, high_ref, slab_ref, first_ref, last_ref, gather_ref
):
    upper = side_ref[0] == 0
    lane = lax.broadcasted_iota(jnp.int32, (GROUP, 128), 1)
    target = jnp.where(upper, 0, 4)
    gather_ref[ROWS:256] = jnp.zeros((256 - ROWS, 128), jnp.float32)

    def sixteen(turn, carry):
        for c in range(3):
            gathered = jnp.zeros((GROUP, 128), jnp.float32)
            for k in range(16):
                rows = velocity_rows(main_ref, low_ref, high_ref, 16 * turn + k, c)
                moved = pltpu.roll(rows, (8 * k + 4) % 128, 1)
                goal = 8 * k + target
                gathered = jnp.where((lane >= goal) & (lane < goal + 4), moved, gathered)
            gather_ref[GROUP * c : GROUP * c + GROUP] = gathered
        slabs = jnp.transpose(gather_ref[...])
        for half in range(2):
            slab_ref[pl.ds(16 * turn, 16), half] = slabs[
                :, 128 * half : 128 * half + 128
            ].reshape(16, 8, 128)
        return carry

    lax.fori_loop(0, 2, sixteen, 0)
    for k in range(7):
        for c in range(3):
            rows = slice(GROUP * c, GROUP * c + GROUP)
            first_ref[k, rows] = velocity_rows(main_ref, low_ref, high_ref, k, c)
            last_ref[k, rows] = velocity_rows(main_ref, low_ref, high_ref, 25 + k, c)


def arrange_velocity(side, main, low, high):
    vmem = pl.BlockSpec(memory_space=pltpu.VMEM)
    smem = pl.BlockSpec(memory_space=pltpu.SMEM)
    return pl.pallas_call(
        velocity_kernel,
        out_shape=(
            jax.ShapeDtypeStruct((32, 2, 8, 128), jnp.float32),
            jax.ShapeDtypeStruct((7, ROWS, 128), jnp.float32),
            jax.ShapeDtypeStruct((7, ROWS, 128), jnp.float32),
        ),
        in_specs=[smem, vmem, vmem, vmem],
        out_specs=(vmem, vmem, vmem),
        scratch_shapes=[pltpu.VMEM((256, 128), jnp.float32)],
        compiler_params=pltpu.CompilerParams(vmem_limit_bytes=16 * 1024 * 1024),
        cost_estimate=pl.CostEstimate(
            flops=4_000_000_000, bytes_accessed=8_000_000, transcendentals=0
        ),
        name="arrange_velocity",
    )(side, main, low, high)


def bands(upper, odd):
    source = lax.broadcasted_iota(jnp.int32, (128, 128), 0)
    target = lax.broadcasted_iota(jnp.int32, (128, 128), 1)

    def entries(distance):
        near = jnp.where(distance == 1, 8.0 if odd else 16.0, 0.0)
        near = jnp.where(distance == -1, -8.0 if odd else 16.0, near)
        near = jnp.where(distance == 2, -1.0, near)
        return jnp.where(distance == -2, 1.0 if odd else -1.0, near)

    main = entries(source - target).astype(jnp.bfloat16)
    layer = source % 8
    begin = jnp.where(upper, 4, 0)
    outer = (layer >= begin) & (layer < begin + 4)
    halo = jnp.where(outer, entries(layer + jnp.where(upper, 124, -4) - target), 0.0)
    return main, halo, source // 8


SCALE_L = 0.1 * 0.5 / 12.0
SCALE_D = 0.1 / 12.0


def fill_bands(upper, even_ref, odd_ref):
    for odd, ref in ((False, even_ref), (True, odd_ref)):
        main, halo, owner = bands(upper, odd)
        for k in range(16):
            ref[k, 0:128] = main
            ref[k, 128:256] = jnp.where(owner == k, halo, 0.0).astype(jnp.bfloat16)


def row_mask(place_ref):
    row = lax.broadcasted_iota(jnp.int32, (GROUP, 128), 0)
    start = jnp.where(place_ref[0] == 0, 8, 0)
    stop = jnp.where(place_ref[0] == place_ref[1] - 1, 72, GROUP)
    return jnp.where((row >= start) & (row < stop), 1.0, 0.0)


def lane_mask(place_ref):
    lane = lax.broadcasted_iota(jnp.int32, (8, 256), 1)
    column = lane % GROUP
    start = jnp.where(place_ref[0] == 0, 8, 0)
    stop = jnp.where(place_ref[0] == place_ref[1] - 1, 72, GROUP)
    mask = jnp.where((column >= start) & (column < stop), 1.0, 0.0)
    return jnp.where(lane < ROWS, mask, 0.0)


def own_slab(near_ref, swapped_ref, plane):
    return jnp.concatenate(
        [
            near_ref[pl.ds(half * PLANES + plane, 8, stride=2 * PLANES), :]
            + swapped_ref[pl.ds(half * PLANES + plane, 8, stride=2 * PLANES), :]
            for half in range(2)
        ],
        1,
    )


def place_mesh(w_ref, a_ref, index, plane, main, slab, upper, inside, inside_slab):
    layer = lax.broadcasted_iota(jnp.int32, (8, 256), 0)
    slab = slab * inside_slab
    a_ref[plane] = slab
    inner = pltpu.roll(slab, 4, 0)
    bottom = jnp.where((layer < 4) & (layer < jnp.where(upper, 0, 8)), inner, main[0:8])
    top = jnp.where((layer >= 4) & (layer < jnp.where(upper, 8, 0)), inner, main[120:128])
    turned = jnp.transpose(jnp.concatenate([bottom, main[8:120], top], 0))
    zeros = jnp.zeros((8, 128), jnp.float32)
    w_ref[index, 0:8] = zeros
    w_ref[index, 248:256] = zeros
    for c in range(3):
        rows = slice(GROUP * c, GROUP * c + GROUP)
        w_ref[index, 8 + GROUP * c : 88 + GROUP * c] = turned[rows] * inside


def place_speed(v_ref, index, main):
    zeros = jnp.zeros((8, 128), jnp.float32)
    v_ref[index, 0:8] = zeros
    v_ref[index, 248:256] = zeros
    v_ref[index, 8:248] = main


def turn_slabs(source_ref, target_ref, groups):
    for g in range(groups):
        stacked = jnp.concatenate([source_ref[16 * g + k] for k in range(16)], 0)
        target_ref[g] = jnp.transpose(stacked)[:ROWS].astype(jnp.bfloat16)


def along_z(main, halo, matrix):
    return jnp.dot(
        jnp.concatenate([main.astype(jnp.bfloat16), halo], 1), matrix,
        preferred_element_type=jnp.float32,
    )


def part(ref, index, c, dx):
    start = 8 + GROUP * c + dx
    return ref[index, start : start + GROUP]


def curvature(ref, at, c):
    near = part(ref, at(1), c, 0) + part(ref, at(-1), c, 0) + (
        part(ref, at(0), c, 1) + part(ref, at(0), c, -1)
    )
    far = part(ref, at(2), c, 0) + part(ref, at(-2), c, 0) + (
        part(ref, at(0), c, 2) + part(ref, at(0), c, -2)
    )
    return 16.0 * near - far


def first_plane(w_ref, w_at, v_ref, v_at, curve, climb, c, centre):
    rows = slice(GROUP * c, GROUP * c + GROUP)
    here = v_at(0)
    slope_x = 8.0 * (part(v_ref, here, c, 1) - part(v_ref, here, c, -1)) - (
        part(v_ref, here, c, 2) - part(v_ref, here, c, -2)
    )
    slope_y = 8.0 * (part(v_ref, v_at(1), c, 0) - part(v_ref, v_at(-1), c, 0)) - (
        part(v_ref, v_at(2), c, 0) - part(v_ref, v_at(-2), c, 0)
    )
    slopes = (slope_x, slope_y, climb[rows])
    stretch = centre[0] * slopes[0] + centre[1] * slopes[1] + centre[2] * slopes[2]
    result = (
        centre[c] * (1.0 - 90.0 * SCALE_L)
        + SCALE_L * (curvature(w_ref, w_at, c) + curve[rows])
        + SCALE_D * stretch
    )
    return result, slopes


def interior_kernel(
    place_ref, grid_ref, near_ref, swapped_ref, main_ref, behind_ref, ahead_ref, slab_ref, slab_other_ref,
    f_ref, d_ref, w_edge_ref,
    w_ref, wt_ref, a_ref, v_ref, vt_ref, b_ref, even_ref, odd_ref,
):
    upper = place_ref[4] == 0
    inside = row_mask(place_ref)
    inside_slab = lane_mask(place_ref)
    fill_bands(upper, even_ref, odd_ref)

    def mesh_plane(plane, carry):
        main = jnp.concatenate(
            [
                grid_ref[pl.ds((16 + half) * PLANES + plane, 128, stride=2 * PLANES), :]
                for half in range(2)
            ],
            1,
        )
        slab = own_slab(near_ref, swapped_ref, plane)
        place_mesh(w_ref, a_ref, plane - 7, plane, main, slab, upper, inside, inside_slab)
        return carry

    blank = jnp.zeros((8, 256), jnp.float32)
    for plane in tuple(range(7)) + tuple(range(33, 48)):
        a_ref[plane] = blank
    for plane in tuple(range(4)) + tuple(range(36, 48)):
        b_ref[plane] = blank
    lax.fori_loop(7, 33, mesh_plane, 0, unroll=2)

    def speed_plane(plane, carry):
        place_speed(
            v_ref, plane,
            jnp.concatenate(
                [velocity_rows(main_ref, behind_ref, ahead_ref, plane, c) for c in range(3)], 0
            ),
        )
        slab = slab_ref[plane] + slab_other_ref[plane]
        b_ref[plane + 4] = jnp.concatenate([slab[0], slab[1]], 1)
        return carry

    lax.fori_loop(0, 32, speed_plane, 0)
    turn_slabs(a_ref, wt_ref, 2)
    turn_slabs(b_ref, vt_ref, 2)
    for k in range(4):
        w_edge_ref[k] = w_ref[k]
        w_edge_ref[4 + k] = w_ref[22 + k]

    def step(k, carry):
        y = k + 9
        curve = along_z(w_ref[y - 7, 8:248], wt_ref[y >> 4], even_ref[y & 15])
        climb = along_z(v_ref[y - 4, 8:248], vt_ref[y >> 4], odd_ref[y & 15])
        zeros = jnp.zeros((8, 128), jnp.float32)
        f_ref[k, 0:8] = zeros
        f_ref[k, 248:256] = zeros
        centre = [part(w_ref, y - 7, c, 0) for c in range(3)]
        for c in range(3):
            result, slopes = first_plane(
                w_ref, lambda o: y - 7 + o, v_ref, lambda o: y - 4 + o, curve, climb, c, centre
            )
            for d in range(3):
                d_ref[k, d, GROUP * c : GROUP * c + GROUP] = slopes[d].astype(jnp.bfloat16)
            f_ref[k, 8 + GROUP * c : 88 + GROUP * c] = result * inside
        return carry

    lax.fori_loop(0, 22, step, 0, unroll=2)


def interior(*arrays):
    vmem = pl.BlockSpec(memory_space=pltpu.VMEM)
    smem = pl.BlockSpec(memory_space=pltpu.SMEM)
    scratch = [
        pltpu.VMEM((26, 256, 128), jnp.float32),
        pltpu.VMEM((2, ROWS, 128), jnp.bfloat16),
        pltpu.VMEM((48, 8, 256), jnp.float32),
        pltpu.VMEM((32, 256, 128), jnp.float32),
        pltpu.VMEM((2, ROWS, 128), jnp.bfloat16),
        pltpu.VMEM((48, 8, 256), jnp.float32),
        pltpu.VMEM((16, 256, 128), jnp.bfloat16),
        pltpu.VMEM((16, 256, 128), jnp.bfloat16),
    ]
    return pl.pallas_call(
        interior_kernel,
        out_shape=(
            jax.ShapeDtypeStruct((22, 256, 128), jnp.float32),
            jax.ShapeDtypeStruct((22, 3, ROWS, 128), jnp.bfloat16),
            jax.ShapeDtypeStruct((8, 256, 128), jnp.float32),
        ),
        in_specs=[smem] + [vmem] * 8,
        out_specs=(vmem,) * 3,
        scratch_shapes=scratch,
        compiler_params=pltpu.CompilerParams(vmem_limit_bytes=34 * 1024 * 1024),
        cost_estimate=pl.CostEstimate(
            flops=15_000_000_000, bytes_accessed=40_000_000, transcendentals=0
        ),
        name="interior",
    )(*arrays)


def edges_kernel(
    place_ref, f_in_ref, d_in_ref, w_edge_ref, speed_low_ref, speed_high_ref,
    near_ref, swapped_ref, slab_ref, slab_other_ref, own_high_ref, own_low_ref, low_ref, high_ref,
    out_ref, w_ref, wt_ref, a_ref, v_ref, vt_ref, b_ref, f_ref, e_ref, even_ref, odd_ref, d_ref, d_mid_ref, done,
):
    copies = [
        pltpu.make_async_copy(f_in_ref, f_ref.at[pl.ds(7, 22)], done.at[0]),
        pltpu.make_async_copy(d_in_ref, d_mid_ref, done.at[1]),
    ]
    for copy in copies:
        copy.start()
    upper = place_ref[4] == 0
    inside = row_mask(place_ref)
    inside_slab = lane_mask(place_ref)
    keep_low = jnp.where(place_ref[2] == 0, 0.0, 1.0)
    keep_high = jnp.where(place_ref[2] == place_ref[3] - 1, 0.0, 1.0)
    fill_bands(upper, even_ref, odd_ref)

    def block(ref, k, start, stop):
        base = 272 * k
        return jnp.concatenate(
            [ref[base + start : base + stop], ref[base + 136 + start : base + 136 + stop]], 1
        )

    for plane in range(7):
        for ref, own_ref, k, own_k, at, keep in (
            (low_ref, own_low_ref, plane, plane - 1, plane, keep_low if plane < 4 else None),
            (high_ref, own_high_ref, plane, plane + 1, plane + 33, keep_high if plane >= 3 else None),
        ):
            main, slab = block(ref, k, 0, 128), block(ref, k, 128, 136)
            if 0 <= own_k < 7:
                main, slab = main + block(own_ref, own_k, 0, 128), slab + block(own_ref, own_k, 128, 136)
            else:
                slab = slab + own_slab(near_ref, swapped_ref, at)
            if keep is not None:
                main, slab = main * keep, slab * keep
            index = at if at < 20 else at - 18
            place_mesh(w_ref, a_ref, index, at, main, slab, upper, inside, inside_slab)
    for k in range(4):
        w_ref[7 + k] = w_edge_ref[k]
        w_ref[11 + k] = w_edge_ref[4 + k]

    def middle_slab(plane, carry):
        a_ref[plane] = own_slab(near_ref, swapped_ref, plane) * inside_slab
        return carry

    lax.fori_loop(7, 33, middle_slab, 0, unroll=2)
    for ref, begin, index in ((low_ref, 0, 0), (high_ref, 36, 18)):
        for k in range(4):
            start, end = 1904 + 240 * k, 2864 + 16 * k
            place_speed(v_ref, index + k, ref[start : start + 240])
            b_ref[begin + k] = jnp.concatenate([ref[end : end + 8], ref[end + 8 : end + 16]], 1)
    for k in range(7):
        place_speed(v_ref, 4 + k, speed_low_ref[k])
        place_speed(v_ref, 11 + k, speed_high_ref[k])

    def speed_slab(plane, carry):
        slab = slab_ref[plane] + slab_other_ref[plane]
        b_ref[plane + 4] = jnp.concatenate([slab[0], slab[1]], 1)
        return carry

    lax.fori_loop(0, 32, speed_slab, 0, unroll=4)
    blank = jnp.zeros((8, 256), jnp.float32)
    for k in range(40, 48):
        a_ref[k] = blank
        b_ref[k] = blank
    turn_slabs(a_ref, wt_ref, 3)
    turn_slabs(b_ref, vt_ref, 3)

    for copy in copies:
        copy.wait()

    def first_steps(start, lag, lag_f, lag_d, keep, outside, stored):
        def step(k, carry):
            y = k + start
            curve = along_z(w_ref[y - lag, 8:248], wt_ref[y >> 4], even_ref[y & 15])
            climb = along_z(v_ref[y - lag, 8:248], vt_ref[y >> 4], odd_ref[y & 15])
            zeros = jnp.zeros((8, 128), jnp.float32)
            scale = jnp.where((k >= outside[0]) & (k < outside[1]), keep, 1.0)
            f_ref[y - lag_f, 0:8] = zeros
            f_ref[y - lag_f, 248:256] = zeros
            centre = [part(w_ref, y - lag, c, 0) for c in range(3)]
            at = lambda o: y - lag + o
            for c in range(3):
                result, slopes = first_plane(w_ref, at, v_ref, at, curve, climb, c, centre)
                for d in range(3):
                    d_ref[y - lag_d, d, GROUP * c : GROUP * c + GROUP] = slopes[d].astype(jnp.bfloat16)
                f_ref[y - lag_f, 8 + GROUP * c : 88 + GROUP * c] = result * (inside * scale)
            return carry

        lax.fori_loop(0, 7, step, 0, unroll=stored)

    first_steps(2, 0, 2, 2, keep_low, (0, 2), 1)
    first_steps(31, 18, 2, 24, keep_high, (5, 7), 1)

    lane = lax.broadcasted_iota(jnp.int32, (8, 256), 1)
    group = lane // GROUP

    def slab_step(k, carry):
        y = k + 4
        here = a_ref[y]
        speed = b_ref[y]

        def both_ways(array, step, axis):
            size = array.shape[axis]
            return pltpu.roll(array, size - step, axis), pltpu.roll(array, step, axis)

        ax1, bx1 = both_ways(here, 1, 1)
        ax2, bx2 = both_ways(here, 2, 1)
        az1, bz1 = both_ways(here, 1, 0)
        az2, bz2 = both_ways(here, 2, 0)
        near = a_ref[y + 1] + a_ref[y - 1] + (ax1 + bx1) + (az1 + bz1)
        far = a_ref[y + 2] + a_ref[y - 2] + (ax2 + bx2) + (az2 + bz2)
        vx1, ux1 = both_ways(speed, 1, 1)
        vx2, ux2 = both_ways(speed, 2, 1)
        vz1, uz1 = both_ways(speed, 1, 0)
        vz2, uz2 = both_ways(speed, 2, 0)
        slope_x = 8.0 * (vx1 - ux1) - (vx2 - ux2)
        slope_y = 8.0 * (b_ref[y + 1] - b_ref[y - 1]) - (b_ref[y + 2] - b_ref[y - 2])
        slope_z = 8.0 * (vz1 - uz1) - (vz2 - uz2)
        right1 = pltpu.roll(here, GROUP, 1)
        right2 = pltpu.roll(here, 2 * GROUP, 1)
        left1 = pltpu.roll(here, 256 - GROUP, 1)
        left2 = pltpu.roll(here, 256 - 2 * GROUP, 1)
        swirl_x = jnp.where(group == 0, here, jnp.where(group == 1, right1, right2))
        swirl_y = jnp.where(group == 0, left1, jnp.where(group == 1, here, right1))
        swirl_z = jnp.where(group == 0, left2, jnp.where(group == 1, left1, here))
        e_ref[k] = (
            here * (1.0 - 90.0 * SCALE_L)
            + SCALE_L * (16.0 * near - far)
            + SCALE_D * (swirl_x * slope_x + swirl_y * slope_y + swirl_z * slope_z)
        )
        return carry

    lax.fori_loop(0, 32, slab_step, 0, unroll=2)
    turn_slabs(e_ref, vt_ref, 2)

    def second(slopes_ref, index, k):
        y = k + 2
        curve = along_z(f_ref[y, 8:248], vt_ref[k >> 4], even_ref[k & 15])
        centre = [part(f_ref, y, c, 0) for c in range(3)]
        for c in range(3):
            rows = slice(GROUP * c, GROUP * c + GROUP)
            slopes = [slopes_ref[index, d, rows].astype(jnp.float32) for d in range(3)]
            stretch = centre[0] * slopes[0] + centre[1] * slopes[1] + centre[2] * slopes[2]
            result = (
                centre[c] * (1.0 - 90.0 * SCALE_L)
                + SCALE_L * (curvature(f_ref, lambda o: y + o, c) + curve[rows])
                + SCALE_D * stretch
            )
            out_ref[pl.ds(2048 * c + k, 64, stride=32), :] = result[8:72]

    def second_low(k, carry):
        second(d_ref, k + 2, k)
        return carry

    def second_high(k, carry):
        second(d_ref, k - 20, k)
        return carry

    def second_middle(k, carry):
        second(d_mid_ref, k - 5, k)
        return carry

    lax.fori_loop(0, 5, second_low, 0)
    lax.fori_loop(27, 32, second_high, 0)
    lax.fori_loop(5, 27, second_middle, 0, unroll=2)


def edges(*arrays):
    vmem = pl.BlockSpec(memory_space=pltpu.VMEM)
    smem = pl.BlockSpec(memory_space=pltpu.SMEM)
    scratch = [
        pltpu.VMEM((22, 256, 128), jnp.float32),
        pltpu.VMEM((3, ROWS, 128), jnp.bfloat16),
        pltpu.VMEM((48, 8, 256), jnp.float32),
        pltpu.VMEM((22, 256, 128), jnp.float32),
        pltpu.VMEM((3, ROWS, 128), jnp.bfloat16),
        pltpu.VMEM((48, 8, 256), jnp.float32),
        pltpu.VMEM((36, 256, 128), jnp.float32),
        pltpu.VMEM((32, 8, 256), jnp.float32),
        pltpu.VMEM((16, 256, 128), jnp.bfloat16),
        pltpu.VMEM((16, 256, 128), jnp.bfloat16),
        pltpu.VMEM((14, 3, ROWS, 128), jnp.bfloat16),
        pltpu.VMEM((22, 3, ROWS, 128), jnp.bfloat16),
        pltpu.SemaphoreType.DMA((2,)),
    ]
    anywhere = pl.BlockSpec(memory_space=pl.ANY)
    return pl.pallas_call(
        edges_kernel,
        out_shape=jax.ShapeDtypeStruct((3 * 64 * 32, 128), jnp.float32),
        in_specs=[smem, anywhere, anywhere] + [vmem] * 11,
        out_specs=vmem,
        scratch_shapes=scratch,
        compiler_params=pltpu.CompilerParams(vmem_limit_bytes=38 * 1024 * 1024),
        name="edges",
    )(*arrays)


def sort_inputs(strength, fraction, stream_cell, span_cell, height_cell):
    key = ((height_cell + 2) << 16) | ((stream_cell + 2) << 8) | (span_cell + 2)
    load = strength.astype(jnp.float32)
    return lax.sort(
        (key, load[0], load[1], load[2], fraction[0], fraction[1], fraction[2]),
        num_keys=1, is_stable=False,
    )


def pack_kernel(key_ref, *refs):
    fields, packed_ref = refs[:6], refs[6]
    key = key_ref[...]
    cells = ((key >> 8) & 255, key & 255, key >> 16)
    for f in range(6):
        packed_ref[64 * f : 64 * f + 64] = fields[f][...]
    for f in range(3):
        packed_ref[384 + 64 * f : 448 + 64 * f] = (cells[f] - 2).astype(jnp.float32)


def pack(parts):
    vmem = pl.BlockSpec(memory_space=pltpu.VMEM)
    return pl.pallas_call(
        pack_kernel,
        out_shape=jax.ShapeDtypeStruct((576, 128), jnp.float32),
        in_specs=[vmem] * 7,
        out_specs=vmem,
        compiler_params=pltpu.CompilerParams(vmem_limit_bytes=16 * 1024 * 1024),
        name="pack",
    )(*[p.reshape(64, 128) for p in parts])


def shards(strength, fraction, stream_cell, span_cell, height_cell, velocity):
    count_x, count_y = lax.axis_size("gx"), lax.axis_size("gy")
    index_x, index_y, index_z = (lax.axis_index(a) for a in ("gx", "gy", "gz"))
    side = index_z.astype(jnp.int32).reshape(1)
    place = jnp.stack(
        [index_x, jnp.int32(count_x), index_y, jnp.int32(count_y), index_z]
    ).astype(jnp.int32)
    up_x = [(i, i + 1) for i in range(count_x - 1)]
    down_x = [(j, i) for i, j in up_x]
    up_y = [(i, i + 1) for i in range(count_y - 1)]
    place, side, velocity = lax.optimization_barrier((place, side, velocity.reshape(6144, 128)))
    upward, downward = cut_velocity(velocity)
    low_speed = lax.ppermute(upward, "gx", up_x)
    high_speed = lax.ppermute(downward, "gx", down_x)
    parts = sort_inputs(strength, fraction, stream_cell, span_cell, height_cell)
    packed = pack(parts)
    low = lax.ppermute(packed, "gx", up_x)
    high = lax.ppermute(packed, "gx", down_x)

    def limits(block):
        span = block[512:576].reshape(32, 256)
        return jnp.stack([span[:, 0], span[:, 255]]).astype(jnp.int32)

    speed_slab, speed_first, speed_last = arrange_velocity(side, velocity, low_speed, high_speed)
    swap = [(0, 1), (1, 0)]
    other_slab = lax.ppermute(speed_slab, "gz", swap)
    bounds = jnp.stack([limits(packed), limits(low), limits(high)])
    grid, near, up_mesh, down_mesh = deposit(bounds, side, packed, low, high)
    swapped = lax.ppermute(near, "gz", swap)
    to_high, to_low = faces(
        up_mesh, down_mesh, near, swapped, speed_first, speed_last, speed_slab, other_slab
    )
    from_low = lax.ppermute(to_high, "gy", up_y)
    from_high = lax.ppermute(to_low, "gy", [(j, i) for i, j in up_y])
    grid = grid.reshape(2 * LAYERS * PLANES, 128)
    middle, slopes, mesh_edges = interior(
        place, grid, near, swapped, velocity, low_speed, high_speed, speed_slab, other_slab
    )
    out = edges(
        place, middle, slopes, mesh_edges, speed_first, speed_last, near, swapped,
        speed_slab, other_slab, to_high, to_low, from_low, from_high,
    )
    return out.reshape(3, 64, 32, 128)


def solution(mesh):
    return jax.shard_map(
        shards,
        mesh=mesh,
        in_specs=(
            P(None, ("gx", "gy", "gz")),
            P(None, ("gx", "gy", "gz")),
            P(("gx", "gy", "gz")),
            P(("gx", "gy", "gz")),
            P(("gx", "gy", "gz")),
            P(None, "gx", "gy", "gz"),
        ),
        out_specs=P(None, "gx", "gy", "gz"),
        check_vma=False,
    )
```

```python
import functools

import jax
import jax.numpy as jnp
from jax import lax
from jax.experimental import pallas as pl
from jax.experimental.pallas import tpu as pltpu
from jax.sharding import PartitionSpec as P

GROUP = 80
ROWS = 240
PLANES = 40
DEPTH = 144
WINDOW = 10
LAYERS = DEPTH + 5


def kernel_weights(fraction):
    remainder = 1.0 - fraction
    return (
        -0.5 * fraction * remainder * remainder,
        1.0 - 2.5 * fraction * fraction + 1.5 * fraction * fraction * fraction,
        1.0 - 2.5 * remainder * remainder + 1.5 * remainder * remainder * remainder,
        -0.5 * fraction * fraction * remainder,
    )


def choose(distance, weights):
    total = jnp.where(distance == 3, weights[3], 0.0)
    for offset in (2, 1, 0):
        total = jnp.where(distance == offset, weights[offset], total)
    return total


def add_source(bounds_ref, number, ref, shift, grid_ref):
    start_x, count_x = {0: (0, GROUP), -64: (0, 16), 64: (64, 16)}[shift]
    rows_x = lax.broadcasted_iota(jnp.int32, (count_x, 128), 0) + start_x
    below = jnp.zeros((start_x, 128), jnp.bfloat16)
    above = jnp.zeros((GROUP - start_x - count_x, 128), jnp.bfloat16)
    rows_y = lax.broadcasted_iota(jnp.int32, (PLANES, 128), 0)
    owner = lax.broadcasted_iota(jnp.int32, (16, 128), 0) // 2

    def group(turn, carry):
        field = [ref[pl.ds(64 * f + 16 * turn, 16), :] for f in range(9)]
        weight_x = kernel_weights(field[3])
        weight_y = kernel_weights(field[4])
        weight_z = kernel_weights(field[5])
        cell_x = field[6].astype(jnp.int32) + (7 + shift)
        cell_y = field[7].astype(jnp.int32) + 3
        cell_z = field[8].astype(jnp.int32) + 7
        low = [bounds_ref[number, 0, 8 * turn + k] + 7 for k in range(8)]
        high = [bounds_ref[number, 1, 8 * turn + k] + 10 for k in range(8)]
        turns = functools.reduce(
            jnp.maximum, [(high[k] - low[k] + WINDOW) // WINDOW for k in range(8)]
        )

        def window(step, inner):
            bases = [jnp.minimum(low[k] + step * WINDOW, DEPTH - 5) for k in range(8)]
            origin = jnp.full((16, 128), bases[0], jnp.int32)
            for k in range(1, 8):
                origin = jnp.where(owner == k, bases[k], origin)
            origin = origin - cell_z
            tall = [choose(origin + j, weight_z) for j in range(WINDOW)]
            for k in range(8):
                leads, crosses = [], []
                for half in (2 * k, 2 * k + 1):
                    row = slice(half, half + 1)
                    spread_x = choose(rows_x - cell_x[row], [w[row] for w in weight_x])
                    spread_y = choose(rows_y - cell_y[row], [w[row] for w in weight_y])
                    leads.append(
                        jnp.concatenate(
                            [
                                part
                                for c in range(3)
                                for part in (
                                    below, (field[c][row] * spread_x).astype(jnp.bfloat16), above
                                )
                                if part.shape[0]
                            ]
                            + [jnp.zeros((16, 128), jnp.bfloat16)],
                            0,
                        )
                    )
                    crosses.append(
                        jnp.concatenate(
                            [
                                jnp.concatenate(
                                    [tall[j][row] * spread_y, tall[j + 1][row] * spread_y], 0
                                ).astype(jnp.bfloat16)
                                for j in range(0, WINDOW, 2)
                            ],
                            0,
                        )
                    )
                product = lax.dot_general(
                    jnp.concatenate(crosses, 1), jnp.concatenate(leads, 1),
                    (((1,), (1,)), ((), ())), preferred_element_type=jnp.float32,
                )
                for j in range(WINDOW):
                    for half in range(2):
                        grid_ref[bases[k] + j, half] += product[
                            PLANES * j : PLANES * j + PLANES, 128 * half : 128 * half + 128
                        ]
            return inner

        lax.fori_loop(0, turns, window, 0)
        return carry

    lax.fori_loop(0, 4, group, 0)


def deposit_kernel(
    bounds_ref, side_ref, own_ref, low_ref, high_ref, grid_ref, near_ref, up_ref, down_ref
):
    def clear(layer, carry):
        grid_ref[layer] = jnp.zeros((2, PLANES, 128), jnp.float32)
        return carry

    lax.fori_loop(0, LAYERS, clear, 0)
    add_source(bounds_ref, 0, own_ref, 0, grid_ref)
    add_source(bounds_ref, 1, low_ref, -64, grid_ref)
    add_source(bounds_ref, 2, high_ref, 64, grid_ref)
    flat_ref = grid_ref.reshape(2 * LAYERS * PLANES, 128)
    inner = jnp.where(side_ref[0] == 0, 132, 4)
    for layer in range(8):
        for half in range(2):
            start = PLANES * (2 * layer + half)
            near_ref[start : start + PLANES] = grid_ref[inner + layer, half]
    for target, plane in ((up_ref, 32), (down_ref, 1)):
        for k in range(7):
            for half in range(2):
                start = 256 * k + 128 * half
                target[start : start + 128] = flat_ref[
                    pl.ds((16 + half) * PLANES + plane + k, 128, stride=2 * PLANES), :
                ]


def deposit(bounds, side, own, low, high):
    vmem = pl.BlockSpec(memory_space=pltpu.VMEM)
    smem = pl.BlockSpec(memory_space=pltpu.SMEM)
    return pl.pallas_call(
        deposit_kernel,
        out_shape=(
            jax.ShapeDtypeStruct((LAYERS, 2, PLANES, 128), jnp.float32),
            jax.ShapeDtypeStruct((16 * PLANES, 128), jnp.float32),
            jax.ShapeDtypeStruct((1792, 128), jnp.float32),
            jax.ShapeDtypeStruct((1792, 128), jnp.float32),
        ),
        in_specs=[smem, smem, vmem, vmem, vmem],
        out_specs=(vmem,) * 4,
        compiler_params=pltpu.CompilerParams(vmem_limit_bytes=24 * 1024 * 1024),
        cost_estimate=pl.CostEstimate(
            flops=16_000_000_000, bytes_accessed=40_000_000, transcendentals=0
        ),
        name="deposit",
    )(bounds, side, own, low, high)


def faces_kernel(
    up_own_ref, down_own_ref, near_ref, swapped_ref, first_ref, last_ref, slab_ref, slab_other_ref,
    up_ref, down_ref,
):
    for target, own, plane, other, speed_ref, skip in (
        (up_ref, up_own_ref, 32, 28, last_ref, 3), (down_ref, down_own_ref, 1, 0, first_ref, 0)
    ):
        for k in range(7):
            for half in range(2):
                start = 272 * k + 136 * half
                first = PLANES * half + plane + k
                block = 256 * k + 128 * half
                target[start : start + 128] = own[block : block + 128]
                target[start + 128 : start + 136] = (
                    near_ref[pl.ds(first, 8, stride=2 * PLANES), :]
                    + swapped_ref[pl.ds(first, 8, stride=2 * PLANES), :]
                )
        for k in range(4):
            target[1904 + 240 * k : 2144 + 240 * k] = speed_ref[skip + k]
            for half in range(2):
                start = 2864 + 16 * k + 8 * half
                target[start : start + 8] = (
                    slab_ref[other + k, half] + slab_other_ref[other + k, half]
                )


def faces(*arrays):
    vmem = pl.BlockSpec(memory_space=pltpu.VMEM)
    return pl.pallas_call(
        faces_kernel,
        out_shape=(jax.ShapeDtypeStruct((2928, 128), jnp.float32),) * 2,
        in_specs=[vmem] * 8,
        out_specs=(vmem, vmem),
        compiler_params=pltpu.CompilerParams(vmem_limit_bytes=24 * 1024 * 1024),
        name="faces",
    )(*arrays)


def cut_kernel(main_ref, up_ref, down_ref, done):
    copies = []
    for c in range(3):
        for k, (target, start) in enumerate(((up_ref, 1920), (down_ref, 0))):
            copies.append(
                pltpu.make_async_copy(
                    main_ref.at[pl.ds(2048 * c + start, 128)],
                    target.at[pl.ds(128 * c, 128)],
                    done.at[2 * c + k],
                )
            )
    for copy in copies:
        copy.start()
    for copy in copies:
        copy.wait()


def cut_velocity(main):
    vmem = pl.BlockSpec(memory_space=pltpu.VMEM)
    return pl.pallas_call(
        cut_kernel,
        out_shape=(jax.ShapeDtypeStruct((384, 128), jnp.float32),) * 2,
        in_specs=[pl.BlockSpec(memory_space=pl.ANY)],
        out_specs=(vmem, vmem),
        scratch_shapes=[pltpu.SemaphoreType.DMA((6,))],
        name="cut_velocity",
    )(main)


def velocity_rows(main_ref, low_ref, high_ref, y, c):
    blank = jnp.zeros((4, 128), jnp.float32)
    return jnp.concatenate(
        [
            blank,
            low_ref[pl.ds(128 * c + y, 4, stride=32), :],
            main_ref[pl.ds(2048 * c + y, 64, stride=32), :],
            high_ref[pl.ds(128 * c + y, 4, stride=32), :],
            blank,
        ],
        0,
    )


def velocity_kernel(
    side_ref, main_ref, low_ref, high_ref, slab_ref, first_ref, last_ref, gather_ref
):
    upper = side_ref[0] == 0
    lane = lax.broadcasted_iota(jnp.int32, (GROUP, 128), 1)
    target = jnp.where(upper, 0, 4)
    gather_ref[ROWS:256] = jnp.zeros((256 - ROWS, 128), jnp.float32)

    def sixteen(turn, carry):
        for c in range(3):
            gathered = jnp.zeros((GROUP, 128), jnp.float32)
            for k in range(16):
                rows = velocity_rows(main_ref, low_ref, high_ref, 16 * turn + k, c)
                moved = pltpu.roll(rows, (8 * k + 4) % 128, 1)
                goal = 8 * k + target
                gathered = jnp.where((lane >= goal) & (lane < goal + 4), moved, gathered)
            gather_ref[GROUP * c : GROUP * c + GROUP] = gathered
        slabs = jnp.transpose(gather_ref[...])
        for half in range(2):
            slab_ref[pl.ds(16 * turn, 16), half] = slabs[
                :, 128 * half : 128 * half + 128
            ].reshape(16, 8, 128)
        return carry

    lax.fori_loop(0, 2, sixteen, 0)
    for k in range(7):
        for c in range(3):
            rows = slice(GROUP * c, GROUP * c + GROUP)
            first_ref[k, rows] = velocity_rows(main_ref, low_ref, high_ref, k, c)
            last_ref[k, rows] = velocity_rows(main_ref, low_ref, high_ref, 25 + k, c)


def arrange_velocity(side, main, low, high):
    vmem = pl.BlockSpec(memory_space=pltpu.VMEM)
    smem = pl.BlockSpec(memory_space=pltpu.SMEM)
    return pl.pallas_call(
        velocity_kernel,
        out_shape=(
            jax.ShapeDtypeStruct((32, 2, 8, 128), jnp.float32),
            jax.ShapeDtypeStruct((7, ROWS, 128), jnp.float32),
            jax.ShapeDtypeStruct((7, ROWS, 128), jnp.float32),
        ),
        in_specs=[smem, vmem, vmem, vmem],
        out_specs=(vmem, vmem, vmem),
        scratch_shapes=[pltpu.VMEM((256, 128), jnp.float32)],
        compiler_params=pltpu.CompilerParams(vmem_limit_bytes=16 * 1024 * 1024),
        cost_estimate=pl.CostEstimate(
            flops=4_000_000_000, bytes_accessed=8_000_000, transcendentals=0
        ),
        name="arrange_velocity",
    )(side, main, low, high)


def bands(upper, odd):
    source = lax.broadcasted_iota(jnp.int32, (128, 128), 0)
    target = lax.broadcasted_iota(jnp.int32, (128, 128), 1)

    def entries(distance):
        near = jnp.where(distance == 1, 8.0 if odd else 16.0, 0.0)
        near = jnp.where(distance == -1, -8.0 if odd else 16.0, near)
        near = jnp.where(distance == 2, -1.0, near)
        return jnp.where(distance == -2, 1.0 if odd else -1.0, near)

    main = entries(source - target).astype(jnp.bfloat16)
    layer = source % 8
    begin = jnp.where(upper, 4, 0)
    outer = (layer >= begin) & (layer < begin + 4)
    halo = jnp.where(outer, entries(layer + jnp.where(upper, 124, -4) - target), 0.0)
    return main, halo, source // 8


SCALE_L = 0.1 * 0.5 / 12.0
SCALE_D = 0.1 / 12.0


def fill_bands(upper, even_ref, odd_ref):
    for odd, ref in ((False, even_ref), (True, odd_ref)):
        main, halo, owner = bands(upper, odd)
        for k in range(16):
            ref[k, 0:128] = main
            ref[k, 128:256] = jnp.where(owner == k, halo, 0.0).astype(jnp.bfloat16)


def row_mask(place_ref):
    row = lax.broadcasted_iota(jnp.int32, (GROUP, 128), 0)
    start = jnp.where(place_ref[0] == 0, 8, 0)
    stop = jnp.where(place_ref[0] == place_ref[1] - 1, 72, GROUP)
    return jnp.where((row >= start) & (row < stop), 1.0, 0.0)


def lane_mask(place_ref):
    lane = lax.broadcasted_iota(jnp.int32, (8, 256), 1)
    column = lane % GROUP
    start = jnp.where(place_ref[0] == 0, 8, 0)
    stop = jnp.where(place_ref[0] == place_ref[1] - 1, 72, GROUP)
    mask = jnp.where((column >= start) & (column < stop), 1.0, 0.0)
    return jnp.where(lane < ROWS, mask, 0.0)


def own_slab(near_ref, swapped_ref, plane):
    return jnp.concatenate(
        [
            near_ref[pl.ds(half * PLANES + plane, 8, stride=2 * PLANES), :]
            + swapped_ref[pl.ds(half * PLANES + plane, 8, stride=2 * PLANES), :]
            for half in range(2)
        ],
        1,
    )


def place_mesh(w_ref, a_ref, index, plane, main, slab, upper, inside, inside_slab):
    layer = lax.broadcasted_iota(jnp.int32, (8, 256), 0)
    slab = slab * inside_slab
    a_ref[plane] = slab
    inner = pltpu.roll(slab, 4, 0)
    bottom = jnp.where((layer < 4) & (layer < jnp.where(upper, 0, 8)), inner, main[0:8])
    top = jnp.where((layer >= 4) & (layer < jnp.where(upper, 8, 0)), inner, main[120:128])
    turned = jnp.transpose(jnp.concatenate([bottom, main[8:120], top], 0))
    zeros = jnp.zeros((8, 128), jnp.float32)
    w_ref[index, 0:8] = zeros
    w_ref[index, 248:256] = zeros
    for c in range(3):
        rows = slice(GROUP * c, GROUP * c + GROUP)
        w_ref[index, 8 + GROUP * c : 88 + GROUP * c] = turned[rows] * inside


def place_speed(v_ref, index, main):
    zeros = jnp.zeros((8, 128), jnp.float32)
    v_ref[index, 0:8] = zeros
    v_ref[index, 248:256] = zeros
    v_ref[index, 8:248] = main


def turn_slabs(source_ref, target_ref, groups):
    for g in range(groups):
        stacked = jnp.concatenate([source_ref[16 * g + k] for k in range(16)], 0)
        target_ref[g] = jnp.transpose(stacked)[:ROWS].astype(jnp.bfloat16)


def along_z(main, halo, matrix):
    return jnp.dot(
        jnp.concatenate([main.astype(jnp.bfloat16), halo], 1), matrix,
        preferred_element_type=jnp.float32,
    )


def part(ref, index, c, dx):
    start = 8 + GROUP * c + dx
    return ref[index, start : start + GROUP]


def curvature(ref, at, c):
    near = part(ref, at(1), c, 0) + part(ref, at(-1), c, 0) + (
        part(ref, at(0), c, 1) + part(ref, at(0), c, -1)
    )
    far = part(ref, at(2), c, 0) + part(ref, at(-2), c, 0) + (
        part(ref, at(0), c, 2) + part(ref, at(0), c, -2)
    )
    return 16.0 * near - far


def first_plane(w_ref, w_at, v_ref, v_at, curve, climb, c, centre):
    rows = slice(GROUP * c, GROUP * c + GROUP)
    here = v_at(0)
    slope_x = 8.0 * (part(v_ref, here, c, 1) - part(v_ref, here, c, -1)) - (
        part(v_ref, here, c, 2) - part(v_ref, here, c, -2)
    )
    slope_y = 8.0 * (part(v_ref, v_at(1), c, 0) - part(v_ref, v_at(-1), c, 0)) - (
        part(v_ref, v_at(2), c, 0) - part(v_ref, v_at(-2), c, 0)
    )
    slopes = (slope_x, slope_y, climb[rows])
    stretch = centre[0] * slopes[0] + centre[1] * slopes[1] + centre[2] * slopes[2]
    result = (
        centre[c] * (1.0 - 90.0 * SCALE_L)
        + SCALE_L * (curvature(w_ref, w_at, c) + curve[rows])
        + SCALE_D * stretch
    )
    return result, slopes


def interior_kernel(
    place_ref, grid_ref, near_ref, swapped_ref, main_ref, behind_ref, ahead_ref, slab_ref, slab_other_ref,
    f_ref, d_ref, w_edge_ref,
    w_ref, wt_ref, a_ref, v_ref, vt_ref, b_ref, even_ref, odd_ref,
):
    upper = place_ref[4] == 0
    inside = row_mask(place_ref)
    inside_slab = lane_mask(place_ref)
    fill_bands(upper, even_ref, odd_ref)

    def mesh_plane(plane, carry):
        main = jnp.concatenate(
            [
                grid_ref[pl.ds((16 + half) * PLANES + plane, 128, stride=2 * PLANES), :]
                for half in range(2)
            ],
            1,
        )
        slab = own_slab(near_ref, swapped_ref, plane)
        place_mesh(w_ref, a_ref, plane - 7, plane, main, slab, upper, inside, inside_slab)
        return carry

    blank = jnp.zeros((8, 256), jnp.float32)
    for plane in tuple(range(7)) + tuple(range(33, 48)):
        a_ref[plane] = blank
    for plane in tuple(range(4)) + tuple(range(36, 48)):
        b_ref[plane] = blank
    lax.fori_loop(7, 33, mesh_plane, 0, unroll=2)

    def speed_plane(plane, carry):
        place_speed(
            v_ref, plane,
            jnp.concatenate(
                [velocity_rows(main_ref, behind_ref, ahead_ref, plane, c) for c in range(3)], 0
            ),
        )
        slab = slab_ref[plane] + slab_other_ref[plane]
        b_ref[plane + 4] = jnp.concatenate([slab[0], slab[1]], 1)
        return carry

    lax.fori_loop(0, 32, speed_plane, 0)
    turn_slabs(a_ref, wt_ref, 2)
    turn_slabs(b_ref, vt_ref, 2)
    for k in range(4):
        w_edge_ref[k] = w_ref[k]
        w_edge_ref[4 + k] = w_ref[22 + k]

    def step(k, carry):
        y = k + 9
        curve = along_z(w_ref[y - 7, 8:248], wt_ref[y >> 4], even_ref[y & 15])
        climb = along_z(v_ref[y - 4, 8:248], vt_ref[y >> 4], odd_ref[y & 15])
        zeros = jnp.zeros((8, 128), jnp.float32)
        f_ref[k, 0:8] = zeros
        f_ref[k, 248:256] = zeros
        centre = [part(w_ref, y - 7, c, 0) for c in range(3)]
        for c in range(3):
            result, slopes = first_plane(
                w_ref, lambda o: y - 7 + o, v_ref, lambda o: y - 4 + o, curve, climb, c, centre
            )
            for d in range(3):
                d_ref[k, d, GROUP * c : GROUP * c + GROUP] = slopes[d].astype(jnp.bfloat16)
            f_ref[k, 8 + GROUP * c : 88 + GROUP * c] = result * inside
        return carry

    lax.fori_loop(0, 22, step, 0, unroll=2)


def interior(*arrays):
    vmem = pl.BlockSpec(memory_space=pltpu.VMEM)
    smem = pl.BlockSpec(memory_space=pltpu.SMEM)
    scratch = [
        pltpu.VMEM((26, 256, 128), jnp.float32),
        pltpu.VMEM((2, ROWS, 128), jnp.bfloat16),
        pltpu.VMEM((48, 8, 256), jnp.float32),
        pltpu.VMEM((32, 256, 128), jnp.float32),
        pltpu.VMEM((2, ROWS, 128), jnp.bfloat16),
        pltpu.VMEM((48, 8, 256), jnp.float32),
        pltpu.VMEM((16, 256, 128), jnp.bfloat16),
        pltpu.VMEM((16, 256, 128), jnp.bfloat16),
    ]
    return pl.pallas_call(
        interior_kernel,
        out_shape=(
            jax.ShapeDtypeStruct((22, 256, 128), jnp.float32),
            jax.ShapeDtypeStruct((22, 3, ROWS, 128), jnp.bfloat16),
            jax.ShapeDtypeStruct((8, 256, 128), jnp.float32),
        ),
        in_specs=[smem] + [vmem] * 8,
        out_specs=(vmem,) * 3,
        scratch_shapes=scratch,
        compiler_params=pltpu.CompilerParams(vmem_limit_bytes=34 * 1024 * 1024),
        cost_estimate=pl.CostEstimate(
            flops=15_000_000_000, bytes_accessed=40_000_000, transcendentals=0
        ),
        name="interior",
    )(*arrays)


def edges_kernel(
    place_ref, f_in_ref, d_in_ref, w_edge_ref, speed_low_ref, speed_high_ref,
    near_ref, swapped_ref, slab_ref, slab_other_ref, own_high_ref, own_low_ref, low_ref, high_ref,
    out_ref, w_ref, wt_ref, a_ref, v_ref, vt_ref, b_ref, f_ref, e_ref, even_ref, odd_ref, d_ref, d_mid_ref, done,
):
    copies = [
        pltpu.make_async_copy(f_in_ref, f_ref.at[pl.ds(7, 22)], done.at[0]),
        pltpu.make_async_copy(d_in_ref, d_mid_ref, done.at[1]),
    ]
    for copy in copies:
        copy.start()
    upper = place_ref[4] == 0
    inside = row_mask(place_ref)
    inside_slab = lane_mask(place_ref)
    keep_low = jnp.where(place_ref[2] == 0, 0.0, 1.0)
    keep_high = jnp.where(place_ref[2] == place_ref[3] - 1, 0.0, 1.0)
    fill_bands(upper, even_ref, odd_ref)

    def block(ref, k, start, stop):
        base = 272 * k
        return jnp.concatenate(
            [ref[base + start : base + stop], ref[base + 136 + start : base + 136 + stop]], 1
        )

    for plane in range(7):
        for ref, own_ref, k, own_k, at, keep in (
            (low_ref, own_low_ref, plane, plane - 1, plane, keep_low if plane < 4 else None),
            (high_ref, own_high_ref, plane, plane + 1, plane + 33, keep_high if plane >= 3 else None),
        ):
            main, slab = block(ref, k, 0, 128), block(ref, k, 128, 136)
            if 0 <= own_k < 7:
                main, slab = main + block(own_ref, own_k, 0, 128), slab + block(own_ref, own_k, 128, 136)
            else:
                slab = slab + own_slab(near_ref, swapped_ref, at)
            if keep is not None:
                main, slab = main * keep, slab * keep
            index = at if at < 20 else at - 18
            place_mesh(w_ref, a_ref, index, at, main, slab, upper, inside, inside_slab)
    for k in range(4):
        w_ref[7 + k] = w_edge_ref[k]
        w_ref[11 + k] = w_edge_ref[4 + k]

    def middle_slab(plane, carry):
        a_ref[plane] = own_slab(near_ref, swapped_ref, plane) * inside_slab
        return carry

    lax.fori_loop(7, 33, middle_slab, 0, unroll=2)
    for ref, begin, index in ((low_ref, 0, 0), (high_ref, 36, 18)):
        for k in range(4):
            start, end = 1904 + 240 * k, 2864 + 16 * k
            place_speed(v_ref, index + k, ref[start : start + 240])
            b_ref[begin + k] = jnp.concatenate([ref[end : end + 8], ref[end + 8 : end + 16]], 1)
    for k in range(7):
        place_speed(v_ref, 4 + k, speed_low_ref[k])
        place_speed(v_ref, 11 + k, speed_high_ref[k])

    def speed_slab(plane, carry):
        slab = slab_ref[plane] + slab_other_ref[plane]
        b_ref[plane + 4] = jnp.concatenate([slab[0], slab[1]], 1)
        return carry

    lax.fori_loop(0, 32, speed_slab, 0, unroll=4)
    blank = jnp.zeros((8, 256), jnp.float32)
    for k in range(40, 48):
        a_ref[k] = blank
        b_ref[k] = blank
    turn_slabs(a_ref, wt_ref, 3)
    turn_slabs(b_ref, vt_ref, 3)

    for copy in copies:
        copy.wait()

    def first_steps(start, lag, lag_f, lag_d, keep, outside, stored):
        def step(k, carry):
            y = k + start
            curve = along_z(w_ref[y - lag, 8:248], wt_ref[y >> 4], even_ref[y & 15])
            climb = along_z(v_ref[y - lag, 8:248], vt_ref[y >> 4], odd_ref[y & 15])
            zeros = jnp.zeros((8, 128), jnp.float32)
            scale = jnp.where((k >= outside[0]) & (k < outside[1]), keep, 1.0)
            f_ref[y - lag_f, 0:8] = zeros
            f_ref[y - lag_f, 248:256] = zeros
            centre = [part(w_ref, y - lag, c, 0) for c in range(3)]
            at = lambda o: y - lag + o
            for c in range(3):
                result, slopes = first_plane(w_ref, at, v_ref, at, curve, climb, c, centre)
                for d in range(3):
                    d_ref[y - lag_d, d, GROUP * c : GROUP * c + GROUP] = slopes[d].astype(jnp.bfloat16)
                f_ref[y - lag_f, 8 + GROUP * c : 88 + GROUP * c] = result * (inside * scale)
            return carry

        lax.fori_loop(0, 7, step, 0, unroll=stored)

    first_steps(2, 0, 2, 2, keep_low, (0, 2), 7)
    first_steps(31, 18, 2, 24, keep_high, (5, 7), 7)

    lane = lax.broadcasted_iota(jnp.int32, (8, 256), 1)
    group = lane // GROUP

    def slab_step(k, carry):
        y = k + 4
        here = a_ref[y]
        speed = b_ref[y]

        def both_ways(array, step, axis):
            size = array.shape[axis]
            return pltpu.roll(array, size - step, axis), pltpu.roll(array, step, axis)

        ax1, bx1 = both_ways(here, 1, 1)
        ax2, bx2 = both_ways(here, 2, 1)
        az1, bz1 = both_ways(here, 1, 0)
        az2, bz2 = both_ways(here, 2, 0)
        near = a_ref[y + 1] + a_ref[y - 1] + (ax1 + bx1) + (az1 + bz1)
        far = a_ref[y + 2] + a_ref[y - 2] + (ax2 + bx2) + (az2 + bz2)
        vx1, ux1 = both_ways(speed, 1, 1)
        vx2, ux2 = both_ways(speed, 2, 1)
        vz1, uz1 = both_ways(speed, 1, 0)
        vz2, uz2 = both_ways(speed, 2, 0)
        slope_x = 8.0 * (vx1 - ux1) - (vx2 - ux2)
        slope_y = 8.0 * (b_ref[y + 1] - b_ref[y - 1]) - (b_ref[y + 2] - b_ref[y - 2])
        slope_z = 8.0 * (vz1 - uz1) - (vz2 - uz2)
        right1 = pltpu.roll(here, GROUP, 1)
        right2 = pltpu.roll(here, 2 * GROUP, 1)
        left1 = pltpu.roll(here, 256 - GROUP, 1)
        left2 = pltpu.roll(here, 256 - 2 * GROUP, 1)
        swirl_x = jnp.where(group == 0, here, jnp.where(group == 1, right1, right2))
        swirl_y = jnp.where(group == 0, left1, jnp.where(group == 1, here, right1))
        swirl_z = jnp.where(group == 0, left2, jnp.where(group == 1, left1, here))
        e_ref[k] = (
            here * (1.0 - 90.0 * SCALE_L)
            + SCALE_L * (16.0 * near - far)
            + SCALE_D * (swirl_x * slope_x + swirl_y * slope_y + swirl_z * slope_z)
        )
        return carry

    lax.fori_loop(0, 32, slab_step, 0, unroll=8)
    turn_slabs(e_ref, vt_ref, 2)

    def second(slopes_ref, index, k):
        y = k + 2
        curve = along_z(f_ref[y, 8:248], vt_ref[k >> 4], even_ref[k & 15])
        centre = [part(f_ref, y, c, 0) for c in range(3)]
        for c in range(3):
            rows = slice(GROUP * c, GROUP * c + GROUP)
            slopes = [slopes_ref[index, d, rows].astype(jnp.float32) for d in range(3)]
            stretch = centre[0] * slopes[0] + centre[1] * slopes[1] + centre[2] * slopes[2]
            result = (
                centre[c] * (1.0 - 90.0 * SCALE_L)
                + SCALE_L * (curvature(f_ref, lambda o: y + o, c) + curve[rows])
                + SCALE_D * stretch
            )
            out_ref[pl.ds(2048 * c + k, 64, stride=32), :] = result[8:72]

    def second_low(k, carry):
        second(d_ref, k + 2, k)
        return carry

    def second_high(k, carry):
        second(d_ref, k - 20, k)
        return carry

    def second_middle(k, carry):
        second(d_mid_ref, k - 5, k)
        return carry

    lax.fori_loop(0, 5, second_low, 0, unroll=5)
    lax.fori_loop(27, 32, second_high, 0, unroll=5)
    lax.fori_loop(5, 27, second_middle, 0, unroll=11)


def edges(*arrays):
    vmem = pl.BlockSpec(memory_space=pltpu.VMEM)
    smem = pl.BlockSpec(memory_space=pltpu.SMEM)
    scratch = [
        pltpu.VMEM((22, 256, 128), jnp.float32),
        pltpu.VMEM((3, ROWS, 128), jnp.bfloat16),
        pltpu.VMEM((48, 8, 256), jnp.float32),
        pltpu.VMEM((22, 256, 128), jnp.float32),
        pltpu.VMEM((3, ROWS, 128), jnp.bfloat16),
        pltpu.VMEM((48, 8, 256), jnp.float32),
        pltpu.VMEM((36, 256, 128), jnp.float32),
        pltpu.VMEM((32, 8, 256), jnp.float32),
        pltpu.VMEM((16, 256, 128), jnp.bfloat16),
        pltpu.VMEM((16, 256, 128), jnp.bfloat16),
        pltpu.VMEM((14, 3, ROWS, 128), jnp.bfloat16),
        pltpu.VMEM((22, 3, ROWS, 128), jnp.bfloat16),
        pltpu.SemaphoreType.DMA((2,)),
    ]
    anywhere = pl.BlockSpec(memory_space=pl.ANY)
    return pl.pallas_call(
        edges_kernel,
        out_shape=jax.ShapeDtypeStruct((3 * 64 * 32, 128), jnp.float32),
        in_specs=[smem, anywhere, anywhere] + [vmem] * 11,
        out_specs=vmem,
        scratch_shapes=scratch,
        compiler_params=pltpu.CompilerParams(vmem_limit_bytes=38 * 1024 * 1024),
        name="edges",
    )(*arrays)


def sort_inputs(strength, fraction, stream_cell, span_cell, height_cell):
    key = ((height_cell + 2) << 16) | ((stream_cell + 2) << 8) | (span_cell + 2)
    load = strength.astype(jnp.float32)
    return lax.sort(
        (key, load[0], load[1], load[2], fraction[0], fraction[1], fraction[2]),
        num_keys=1, is_stable=False,
    )


def pack_kernel(key_ref, *refs):
    fields, packed_ref = refs[:6], refs[6]
    key = key_ref[...]
    cells = ((key >> 8) & 255, key & 255, key >> 16)
    for f in range(6):
        packed_ref[64 * f : 64 * f + 64] = fields[f][...]
    for f in range(3):
        packed_ref[384 + 64 * f : 448 + 64 * f] = (cells[f] - 2).astype(jnp.float32)


def pack(parts):
    vmem = pl.BlockSpec(memory_space=pltpu.VMEM)
    return pl.pallas_call(
        pack_kernel,
        out_shape=jax.ShapeDtypeStruct((576, 128), jnp.float32),
        in_specs=[vmem] * 7,
        out_specs=vmem,
        compiler_params=pltpu.CompilerParams(vmem_limit_bytes=16 * 1024 * 1024),
        name="pack",
    )(*[p.reshape(64, 128) for p in parts])


def shards(strength, fraction, stream_cell, span_cell, height_cell, velocity):
    count_x, count_y = lax.axis_size("gx"), lax.axis_size("gy")
    index_x, index_y, index_z = (lax.axis_index(a) for a in ("gx", "gy", "gz"))
    side = index_z.astype(jnp.int32).reshape(1)
    place = jnp.stack(
        [index_x, jnp.int32(count_x), index_y, jnp.int32(count_y), index_z]
    ).astype(jnp.int32)
    up_x = [(i, i + 1) for i in range(count_x - 1)]
    down_x = [(j, i) for i, j in up_x]
    up_y = [(i, i + 1) for i in range(count_y - 1)]
    place, side, velocity = lax.optimization_barrier((place, side, velocity.reshape(6144, 128)))
    upward, downward = cut_velocity(velocity)
    low_speed = lax.ppermute(upward, "gx", up_x)
    high_speed = lax.ppermute(downward, "gx", down_x)
    parts = sort_inputs(strength, fraction, stream_cell, span_cell, height_cell)
    packed = pack(parts)
    low = lax.ppermute(packed, "gx", up_x)
    high = lax.ppermute(packed, "gx", down_x)

    def limits(block):
        span = block[512:576].reshape(32, 256)
        return jnp.stack([span[:, 0], span[:, 255]]).astype(jnp.int32)

    speed_slab, speed_first, speed_last = arrange_velocity(side, velocity, low_speed, high_speed)
    swap = [(0, 1), (1, 0)]
    other_slab = lax.ppermute(speed_slab, "gz", swap)
    bounds = jnp.stack([limits(packed), limits(low), limits(high)])
    grid, near, up_mesh, down_mesh = deposit(bounds, side, packed, low, high)
    swapped = lax.ppermute(near, "gz", swap)
    to_high, to_low = faces(
        up_mesh, down_mesh, near, swapped, speed_first, speed_last, speed_slab, other_slab
    )
    from_low = lax.ppermute(to_high, "gy", up_y)
    from_high = lax.ppermute(to_low, "gy", [(j, i) for i, j in up_y])
    grid = grid.reshape(2 * LAYERS * PLANES, 128)
    middle, slopes, mesh_edges = interior(
        place, grid, near, swapped, velocity, low_speed, high_speed, speed_slab, other_slab
    )
    out = edges(
        place, middle, slopes, mesh_edges, speed_first, speed_last, near, swapped,
        speed_slab, other_slab, to_high, to_low, from_low, from_high,
    )
    return out.reshape(3, 64, 32, 128)


def solution(mesh):
    return jax.shard_map(
        shards,
        mesh=mesh,
        in_specs=(
            P(None, ("gx", "gy", "gz")),
            P(None, ("gx", "gy", "gz")),
            P(("gx", "gy", "gz")),
            P(("gx", "gy", "gz")),
            P(("gx", "gy", "gz")),
            P(None, "gx", "gy", "gz"),
        ),
        out_specs=P(None, "gx", "gy", "gz"),
        check_vma=False,
    )
```
